256 devices in a mesh: unit: 4 (over x), samp: 64 (over z, y, core).
Axes of the slice: x: 4, y: 4, z: 8, core: 2. Of those that a mesh axis runs over, the one named last changes fastest.
Arguments:
- states: float32 [65536, 8192], P('samp', 'unit'), may hold values from -0.0234375 to 0.0234375
- targets: float32 [65536, 64], P('samp'), may hold values from -6 to 6
Outputs:
- readout: float32 [8192, 64], P('unit')
- residual: float32 [65536, 64], P('samp')
The draws below stay inside these ranges and needn't reach their ends.
All inputs are finite; a program needn't handle non-finite values.
Results may differ from the reference program's by a relative error of at most 0.0003.
Values sent between devices are 32-bit elements; how exact they have to be, the bound alone decides.
No kernel may reach another device: no remote copies, remote signals or barrier semaphores. Data moves between devices by JAX's collectives and lax.ppermute only.
A program may use at most 64 MiB of HBM per device.

```python
import jax
import jax.numpy as jnp
from jax import lax

U = 8192
O = 64
ITERS = 3
SAMPLES = 65536


def steps_of(key, dims, split, least, largest):
    gain = 1.0
    for dim, blocks in split:
        heights = jax.random.uniform(jax.random.fold_in(jax.random.fold_in(key, 6), dim), (blocks,), jnp.float32, least / len(split), largest / len(split))
        gain = gain * jnp.repeat(jnp.exp(heights), dims[dim] // blocks).reshape((-1,) + (1,) * (len(dims) - 1 - dim))
    return gain


def bell_draw(own_key, shape, width, limit, split=(), kind=jnp.bfloat16):
    values = jax.random.normal(own_key, shape, jnp.float32) * width
    if len(split) > 0:
        values = steps_of(own_key, shape, split, -0.22, 0.18) * values
    return jnp.clip(values, min=-limit, max=limit).astype(kind)


def setup_inputs(seed: int = 0) -> dict:
    seeds = jax.random.split(jax.random.key(seed), 3)
    states = bell_draw(seeds[0], (SAMPLES, U), SAMPLES ** -0.5, 0.0234375, ((0, 64), (1, 4)), jnp.float32)
    targets = bell_draw(seeds[1], (SAMPLES, O), 1.0, 6.0, ((0, 64),), jnp.float32)
    return dict(states=states, targets=targets)


ridge = 0.5


def transposed(states, residual):
    return lax.dot_general(states, residual, (((0,), (0,)), ((), ())), precision=lax.Precision.HIGHEST, preferred_element_type=jnp.float32)


def reference(states, targets):
    readout = jnp.zeros((states.shape[1], targets.shape[1]), jnp.float32)
    residual = targets
    gradient = transposed(states, residual) - ridge * readout
    direction = gradient
    gamma = jnp.sum(gradient * gradient)
    for step in range(ITERS):
        image = jnp.dot(states, direction, precision=lax.Precision.HIGHEST, preferred_element_type=jnp.float32)
        delta = jnp.sum(image * image) + ridge * jnp.sum(direction * direction)
        alpha = gamma / delta
        readout = readout + alpha * direction
        residual = residual - alpha * image
        if step + 1 < ITERS:
            gradient = transposed(states, residual) - ridge * readout
            gamma_next = jnp.sum(gradient * gradient)
            direction = gradient + (gamma_next / gamma) * direction
            gamma = gamma_next
    return readout, residual
```

```python
import jax
import jax.numpy as jnp
from jax import lax
from jax.sharding import PartitionSpec as P

ITERS = 3
ridge = 0.5
Y, CORES, LANES = 4, 2, 128


def rounded(values):
    return lax.reduce_precision(values, 8, 7)


def split2(values):
    high = rounded(values)
    return high.astype(jnp.bfloat16), rounded(values - high).astype(jnp.bfloat16)


def split3(values):
    high = rounded(values)
    rest = values - high
    middle = rounded(rest)
    parts = [high, middle, rounded(rest - middle)]
    return jnp.concatenate(parts, axis=0).astype(jnp.bfloat16)


def product(rows, states_parts, contract):
    stacked = split3(rows)
    total = 0.0
    for part in states_parts[::-1]:
        p = lax.dot_general(
            stacked,
            part,
            (((1,), (contract,)), ((), ())),
            preferred_element_type=jnp.float32,
        )
        n = rows.shape[0]
        total = total + (p[2 * n :] + p[n : 2 * n] + p[:n])
    return total


def shards(states, targets):
    units = states.shape[1]
    samples, outputs = targets.shape
    samp_count = lax.axis_size("samp")
    chips = samp_count // CORES
    half = outputs // CORES
    core = lax.axis_index("samp") % CORES

    swap_cores = [(i, i ^ 1) for i in range(samp_count)]
    groups = [[chip * CORES + c for chip in range(chips)] for c in range(CORES)]

    def swap(x):
        return lax.ppermute(x, "samp", swap_cores)

    def exchange(x):
        return lax.all_to_all(x, "samp", 0, 0, axis_index_groups=groups, tiled=True)

    def unit_hop(x, mask):
        return lax.ppermute(x, "unit", [(i, i ^ mask) for i in range(lax.axis_size("unit"))])

    def unit_sum(a, b):
        a, b = a + unit_hop(a, 1), b + unit_hop(b, 3)
        return a + unit_hop(a, 3), b + unit_hop(b, 1)

    def turn(x):
        return jnp.where(core == 0, x, jnp.concatenate([x[half:], x[:half]], axis=0))

    parts = split2(states)

    def scatter_sum(residual, scalar):
        g = product(residual, parts, 0).reshape(outputs, units // LANES, LANES)
        extra = jnp.broadcast_to(scalar, (half, 1, LANES))
        mine = jnp.concatenate([g[:half], extra], axis=1)
        theirs = jnp.concatenate([g[half:], extra], axis=1)
        mine = mine + swap(theirs)
        rows = mine.shape[1]
        got = exchange(mine.reshape(half * rows, 1, LANES)).reshape(half, rows, LANES)
        got = jnp.sum(got, axis=0)
        return got[: rows - 1], got[rows - 1, 0]

    def gather(shard):
        mine = exchange(jnp.broadcast_to(shard[None], (half,) + shard.shape))
        return jnp.concatenate([mine, swap(mine)], axis=0).reshape(outputs, units)

    def image_sum(g, scalars):
        p = product(g, parts, 1).reshape(outputs * samples // LANES, LANES)
        n = p.shape[0] // 2
        tile = jnp.concatenate(
            [jnp.broadcast_to(s, (1, LANES)) for s in scalars]
            + [jnp.zeros((8 - len(scalars), LANES), jnp.float32)],
            axis=0,
        )
        a, b = unit_sum(jnp.concatenate([p[:n], tile], axis=0), p[n:])
        image = jnp.concatenate([a[:n], b], axis=0).reshape(outputs, samples)
        return image, [a[n + i, 0] for i in range(len(scalars))]

    residual = turn(targets.T)
    shard, _ = scatter_sum(residual, jnp.float32(0))
    gradient = gather(shard)
    readout = jnp.zeros_like(gradient)
    direction = gradient
    shard_direction = shard
    for step in range(ITERS):
        square = jnp.sum(gradient * gradient)
        if step == 0:
            image, (gamma,) = image_sum(gradient, [square])
            direction_sq = gamma
        else:
            cross = jnp.sum(gradient * direction)
            new_image, (gamma_next, cross) = image_sum(gradient, [square, cross])
            beta = gamma_next / gamma
            gamma = gamma_next
            image = new_image + beta * image
            direction = gradient + beta * direction
            shard_direction = shard + beta * shard_direction
            direction_sq = gamma + beta * (2.0 * cross + beta * direction_sq)
        image_sq = jnp.sum(image * image)
        if step + 1 < ITERS:
            back, image_sq = scatter_sum(image, image_sq)
            alpha = gamma / (image_sq + ridge * direction_sq)
            shard = shard - alpha * (back + ridge * shard_direction)
            gradient = gather(shard)
        else:
            tile = jnp.broadcast_to(image_sq, (chips, 1, LANES))
            got = exchange(tile + swap(tile))
            image_sq = jnp.sum(got[:, 0, 0])
            alpha = gamma / (image_sq + ridge * direction_sq)
        readout = readout + alpha * direction
        residual = residual - alpha * image
    return turn(readout).T, turn(residual).T


def solution(mesh):
    return jax.shard_map(
        shards,
        mesh=mesh,
        in_specs=(P("samp", "unit"), P("samp", None)),
        out_specs=(P("unit", None), P("samp", None)),
        check_vma=False,
    )
```

```python
import functools

import jax
import jax.numpy as jnp
from jax import lax
from jax.experimental import pallas as pl
from jax.experimental.pallas import tpu as pltpu
from jax.sharding import PartitionSpec as P

ITERS = 3
ridge = 0.5
CORES, LANES, TILE = 2, 128, 8
WIDE = 256
MIB = 1 << 20
F32, BF16 = jnp.float32, jnp.bfloat16
VMEM = pl.BlockSpec(memory_space=pltpu.VMEM)
HBM = pl.BlockSpec(memory_space=pl.ANY)


def shape(*dims, dtype=F32):
    return jax.ShapeDtypeStruct(dims, dtype)


def here(x):
    return pltpu.with_memory_space_constraint(x, pltpu.VMEM)


def call(kernel, out_shape, *args, scratch=(), limit=24, specs=None, flops=0, **static):
    return pl.pallas_call(
        functools.partial(kernel, **static),
        in_specs=specs or [VMEM] * len(args),
        out_specs=jax.tree.map(lambda _: VMEM, out_shape),
        out_shape=out_shape,
        scratch_shapes=list(scratch),
        compiler_params=pltpu.CompilerParams(vmem_limit_bytes=limit * MIB),
        cost_estimate=pl.CostEstimate(flops=flops, bytes_accessed=MIB, transcendentals=0),
        name=kernel.__name__,
    )(*args)


def split3(x):
    high = x.astype(BF16)
    rest = x - high.astype(F32)
    middle = rest.astype(BF16)
    low = (rest - middle.astype(F32)).astype(BF16)
    return jnp.concatenate([high, middle, low], axis=0)


def dot(a, b, ca, cb):
    return lax.dot_general(a, b, (((ca,), (cb,)), ((), ())), preferred_element_type=F32)


def fold3(p):
    n = p.shape[0] // 3
    return p[2 * n :] + p[n : 2 * n] + p[:n]


def row(x):
    return jnp.broadcast_to(x, (1, LANES))


def store_pieces(mine, theirs, value, at, stride):
    half = value.shape[0] // CORES
    for i in range(WIDE // LANES):
        part = value[:, i * LANES : (i + 1) * LANES]
        j = at * (WIDE // LANES) + i
        mine[pl.ds(j, half, stride=stride), :] = part[:half]
        theirs[pl.ds(j, half, stride=stride), :] = part[half:]


def first(core, states, targets, high, low, turned, mine, theirs, buf, sems):
    steps = buf.shape[0]
    copies = [
        pltpu.make_async_copy(
            states.at[:, pl.ds(t * WIDE, WIDE)], buf.at[t], sems.at[t]
        )
        for t in range(steps)
    ]
    for c in copies:
        c.start()
    half = targets.shape[0] // CORES
    own = core[0, 0] == 0
    top, bottom = targets[:half, :], targets[half:, :]
    x = jnp.concatenate(
        [jnp.where(own, top, bottom), jnp.where(own, bottom, top)], axis=0
    )
    turned[...] = x
    x3 = split3(x)
    for t in range(steps):
        copies[t].wait()
        s = buf[t]
        h = s.astype(BF16)
        l = (s - h.astype(F32)).astype(BF16)
        high[:, pl.ds(t * WIDE, WIDE)] = h
        low[:, pl.ds(t * WIDE, WIDE)] = l
        store_pieces(mine, theirs, fold3(dot(x3, l, 1, 0) + dot(x3, h, 1, 0)), t, mine.shape[0] // half)


def combine(a, ra, b, rb):
    n = b.shape[0]
    image = jnp.concatenate([a[:n, :] + ra[:n, :], b[...] + rb[...]], axis=1)
    tail = a[n : n + TILE, :LANES] + ra[n : n + TILE, :LANES]
    return image, tail


def step_image(a, ra, b, rb, before, scal, image_out, scal_out):
    image, tail = combine(a, ra, b, rb)
    gamma = tail[0:1]
    if before is None:
        beta = jnp.zeros_like(gamma)
        square = gamma
    else:
        beta = gamma / scal[0:1, :]
        square = gamma + beta * (2.0 * tail[1:2] + beta * scal[2:3, :])
        image = image + beta[:, :1] * before[...]
    image_out[...] = image
    scal_out[0:1, :] = gamma
    scal_out[1:2, :] = beta
    scal_out[2:3, :] = square
    scal_out[3:, :] = jnp.zeros((TILE - 3, LANES), F32)
    return image, row(jnp.sum(image * image))


def back(*refs, later):
    if later:
        a, ra, b, rb, before, scal, high, low, image_out, scal_out, mine, theirs = refs
    else:
        a, ra, b, rb, high, low, image_out, scal_out, mine, theirs = refs
        before = scal = None
    image, image_sq = step_image(a, ra, b, rb, before, scal, image_out, scal_out)
    half = image.shape[0] // CORES
    stride = mine.shape[0] // half
    x3 = split3(image)
    for t in range(high.shape[1] // WIDE):
        at = pl.ds(t * WIDE, WIDE)
        p = dot(x3, low[:, at], 1, 0) + dot(x3, high[:, at], 1, 0)
        store_pieces(mine, theirs, fold3(p), t, stride)
    extra = jnp.broadcast_to(image_sq, (half, LANES))
    mine[pl.ds(stride - 1, half, stride=stride), :] = extra
    theirs[pl.ds(stride - 1, half, stride=stride), :] = extra


def last_image(a, ra, b, rb, before, scal, image_out, scal_out, squares):
    _, image_sq = step_image(a, ra, b, rb, before, scal, image_out, scal_out)
    squares[...] = jnp.broadcast_to(image_sq, squares.shape)


def step_size(image_sq, scal):
    return scal[0:1, :] / (image_sq + ridge * scal[2:3, :])


def reduce_pieces(*refs, rows, scalars):
    if scalars:
        got, scal, out, size = refs
    else:
        got, out = refs
    count = out.shape[0] // rows
    stride = got.shape[0] // count
    terms = [got[i * stride : (i + 1) * stride, :] for i in range(count)]
    while len(terms) > 1:
        terms = [terms[i] + terms[i + 1] for i in range(0, len(terms), 2)]
    total = terms[0]
    for i in range(count):
        out[i * rows : (i + 1) * rows, :] = total[:rows]
    if scalars:
        size[...] = jnp.broadcast_to(step_size(total[rows : rows + 1], scal), size.shape)


def forward(*refs, step):
    if step == 0:
        top, bottom, high, low, gradient, a, b = refs
        g = jnp.concatenate([top[...], bottom[...]], axis=0)
        cross = None
    else:
        if step == 1:
            top, bottom, size, scal, g_old, high, low, gradient, direction, a, b = refs
            d = g_old[...]
        else:
            top, bottom, size, scal, g_old, d_old, high, low, gradient, direction, a, b = refs
            d = g_old[...] + scal[1:2, :] * d_old[...]
        q = jnp.concatenate([top[...], bottom[...]], axis=0)
        direction[...] = d
        g = g_old[...] - size[0:1, :] * (q + ridge * d)
        cross = jnp.sum(g * d)
    gradient[...] = g
    n = b.shape[0]
    stride = g.shape[0] // n
    a[n : n + 1, :] = jnp.broadcast_to(jnp.sum(g * g), (1, a.shape[1]))
    rest = jnp.zeros((TILE - 1, a.shape[1]), F32)
    a[n + 1 : n + TILE, :] = rest if cross is None else rest + cross
    x3 = split3(
        jnp.concatenate([gradient[pl.ds(j, n, stride=stride), :] for j in range(stride)], axis=1)
    )
    for t in range(high.shape[0] // WIDE):
        at = pl.ds(t * WIDE, WIDE)
        p = fold3(dot(x3, low[at, :], 1, 1) + dot(x3, high[at, :], 1, 1))
        out, k = (a, t) if t < a.shape[1] // WIDE else (b, t - a.shape[1] // WIDE)
        out[0:n, k * WIDE : (k + 1) * WIDE] = p


def finish(core, got, other, scal, size0, size1, d0, d1, g2, i0, i1, i2, targets, readout, residual, sums):
    n = targets.shape[0]
    half = n // CORES
    stride = d0.shape[0] // n
    image_sq = jnp.sum(got[...] + other[...], axis=0, keepdims=True)
    size2 = step_size(image_sq, scal)
    own = core[0, 0] == 0
    s0, s1 = size0[0:1, :], size1[0:1, :]
    direction = g2[...] + scal[1:2, :] * d1[...]
    total = s0 * d0[...] + s1 * d1[...] + size2 * direction
    sums[...] = total
    for j in range(stride):
        x = sums[pl.ds(j, n, stride=stride), :]
        at = pl.ds(j * LANES, LANES)
        readout[:half, at] = jnp.where(own, x[:half], x[half:])
        readout[half:, at] = jnp.where(own, x[half:], x[:half])
    r = targets[...] - s0[:, :1] * i0[...] - s1[:, :1] * i1[...] - size2[:, :1] * i2[...]
    residual[:half, :] = jnp.where(own, r[:half], r[half:])
    residual[half:, :] = jnp.where(own, r[half:], r[:half])


def shards(states, targets):
    samples, units = states.shape
    outputs = targets.shape[1]
    samp_count = lax.axis_size("samp")
    unit_count = lax.axis_size("unit")
    chips = samp_count // CORES
    half = outputs // CORES
    rows = units // LANES
    core = jnp.full((1, 1), lax.axis_index("samp") % CORES, jnp.int32)

    swap_cores = [(i, i ^ 1) for i in range(samp_count)]
    groups = [[chip * CORES + c for chip in range(chips)] for c in range(CORES)]

    def swap(x):
        return lax.ppermute(x, "samp", swap_cores)

    def exchange(x):
        n = x.shape[0]
        x = x.reshape(n, 1, LANES)
        x = lax.all_to_all(x, "samp", 0, 0, axis_index_groups=groups, tiled=True)
        return x.reshape(n, LANES)

    def unit_hop(x, mask):
        return lax.ppermute(x, "unit", [(i, i ^ mask) for i in range(unit_count)])

    def unit_sum(a, b):
        a, b = a + unit_hop(a, 1), b + unit_hop(b, 3)
        return a, unit_hop(a, 3), b, unit_hop(b, 1)

    vector = shape(TILE, LANES)
    image_shape = shape(outputs, samples)
    whole = shape(outputs * rows, LANES)
    ab = [shape(outputs + TILE, samples // 2), shape(outputs, samples // 2)]
    flops = 2 * 6 * samples * units * outputs

    smem = pl.BlockSpec(memory_space=pltpu.SMEM)
    high, low, turned, mine, theirs = call(
        first,
        [shape(samples, units, dtype=BF16)] * 2 + [image_shape] + [shape(half * rows, LANES)] * 2,
        core,
        states,
        here(targets.T),
        specs=[smem, HBM, VMEM],
        scratch=[
            pltpu.VMEM((units // WIDE, samples, WIDE), F32),
            pltpu.SemaphoreType.DMA((units // WIDE,)),
        ],
        limit=32,
        flops=flops,
    )
    high, low = here(high), here(low)
    got = exchange(mine + swap(theirs))
    spread = call(reduce_pieces, shape(half * rows, LANES), got, rows=rows, scalars=False)

    gradients, directions, images, sizes = [], [], [], []
    scal = size = None
    for step in range(ITERS):
        top = exchange(spread)
        bottom = swap(top)
        if step == 0:
            g, a, b = call(forward, [whole] + ab, top, bottom, high, low, step=0, flops=flops)
        else:
            olds = [gradients[-1]] + ([directions[-1]] if step > 1 else [])
            g, d, a, b = call(
                forward,
                [whole, whole] + ab,
                top,
                bottom,
                size,
                scal,
                *olds,
                high,
                low,
                step=step,
                flops=flops,
            )
            directions.append(d)
        gradients.append(g)
        hops = unit_sum(a, b)
        olds = [images[-1], scal] if step else []
        if step + 1 < ITERS:
            piece = shape(half * (rows + 1), LANES)
            image, scal, mine, theirs = call(
                back,
                [image_shape, vector, piece, piece],
                *hops,
                *olds,
                high,
                low,
                later=step > 0,
                flops=flops,
            )
            images.append(image)
            got = exchange(mine + swap(theirs))
            spread, size = call(
                reduce_pieces,
                [shape(half * rows, LANES), vector],
                got,
                scal,
                rows=rows,
                scalars=True,
            )
            sizes.append(size)
        else:
            image, scal, squares = call(
                last_image, [image_shape, vector, shape(half, LANES)], *hops, *olds
            )
            images.append(image)
            got = exchange(squares)
            other = swap(got)
    readout, residual = call(
        finish,
        [shape(outputs, units), image_shape],
        core,
        got,
        other,
        scal,
        *sizes,
        *directions,
        gradients[-1],
        *images,
        turned,
        specs=[smem] + [VMEM] * 12,
        scratch=[pltpu.VMEM((outputs * rows, LANES), F32)],
    )
    return readout.T, residual.T


def solution(mesh):
    return jax.shard_map(
        shards,
        mesh=mesh,
        in_specs=(P("samp", "unit"), P("samp", None)),
        out_specs=(P("unit", None), P("samp", None)),
        check_vma=False,
    )
```

```python
import functools

import jax
import jax.numpy as jnp
from jax import lax
from jax.experimental import pallas as pl
from jax.experimental.pallas import tpu as pltpu
from jax.sharding import PartitionSpec as P

ITERS = 3
ridge = 0.5
CORES, LANES, TILE = 2, 128, 8
WIDE = 256
MIB = 1 << 20
F32, BF16 = jnp.float32, jnp.bfloat16
VMEM = pl.BlockSpec(memory_space=pltpu.VMEM)
HBM = pl.BlockSpec(memory_space=pl.ANY)


def shape(*dims, dtype=F32):
    return jax.ShapeDtypeStruct(dims, dtype)


def here(x):
    return pltpu.with_memory_space_constraint(x, pltpu.VMEM)


def call(kernel, out_shape, *args, scratch=(), limit=24, specs=None, flops=0, **static):
    return pl.pallas_call(
        functools.partial(kernel, **static),
        in_specs=specs or [VMEM] * len(args),
        out_specs=jax.tree.map(lambda _: VMEM, out_shape),
        out_shape=out_shape,
        scratch_shapes=list(scratch),
        compiler_params=pltpu.CompilerParams(vmem_limit_bytes=limit * MIB),
        cost_estimate=pl.CostEstimate(flops=flops, bytes_accessed=MIB, transcendentals=0),
        name=kernel.__name__,
    )(*args)


def split2(x):
    high = x.astype(BF16)
    return jnp.concatenate([high, (x - high.astype(F32)).astype(BF16)], axis=0)


def dot(a, b, ca, cb):
    return lax.dot_general(a, b, (((ca,), (cb,)), ((), ())), preferred_element_type=F32)


def fold(p):
    n = p.shape[0] // 2
    return p[n:] + p[:n]


def rows_product(x, high, low, at):
    x2 = split2(x) if x.dtype == F32 else x
    return fold(dot(x2, low[:, at], 1, 0) + dot(x2, high[:, at], 1, 0))


def row(x):
    return jnp.broadcast_to(x, (1, LANES))


def store_pieces(mine, theirs, value, at, stride):
    half = value.shape[0] // CORES
    for i in range(WIDE // LANES):
        part = value[:, i * LANES : (i + 1) * LANES]
        j = at * (WIDE // LANES) + i
        mine[pl.ds(j, half, stride=stride), :] = part[:half]
        theirs[pl.ds(j, half, stride=stride), :] = part[half:]


def own_half_first(x, own):
    half = x.shape[0] // CORES
    top, bottom = x[:half], x[half:]
    return jnp.concatenate(
        [jnp.where(own, top, bottom), jnp.where(own, bottom, top)], axis=0
    )


def first(core, states, targets, high, low, turned, mine, theirs, buf, target_buf, sems):
    steps = buf.shape[0]
    fetch = pltpu.make_async_copy(targets, target_buf, sems.at[steps])
    fetch.start()
    copies = [
        pltpu.make_async_copy(
            states.at[:, pl.ds(t * WIDE, WIDE)], buf.at[t], sems.at[t]
        )
        for t in range(steps)
    ]
    for c in copies:
        c.start()
    fetch.wait()
    x = own_half_first(target_buf[...], core[0, 0] == 0)
    turned[...] = x
    x2 = split2(x)
    half = x.shape[0] // CORES
    for t in range(steps):
        copies[t].wait()
        s = buf[t]
        h = s.astype(BF16)
        l = (s - h.astype(F32)).astype(BF16)
        high[:, pl.ds(t * WIDE, WIDE)] = h
        low[:, pl.ds(t * WIDE, WIDE)] = l
        p = fold(dot(x2, l, 1, 0) + dot(x2, h, 1, 0))
        store_pieces(mine, theirs, p, t, mine.shape[0] // half)


def turn_states(high, low, high_turned, low_turned):
    high_turned[...] = high[...].T
    low_turned[...] = low[...].T


def combine(hops):
    p = hops[0][...] + hops[1][...] + (hops[2][...] + hops[3][...])
    n = p.shape[0] - TILE
    return p[:n], p[n:, :LANES]


def step_image(hops, before, scal, image_out, scal_out):
    image, tail = combine(hops)
    gamma = tail[0:1]
    if before is None:
        beta = jnp.zeros_like(gamma)
        square = gamma
    else:
        beta = gamma / scal[0:1, :]
        square = gamma + beta * (2.0 * tail[1:2] + beta * scal[2:3, :])
        image = image + beta[:, :1] * before[...]
    image_out[...] = image
    scal_out[0:1, :] = gamma
    scal_out[1:2, :] = beta
    scal_out[2:3, :] = square
    scal_out[3:, :] = jnp.zeros((TILE - 3, LANES), F32)
    return image, row(jnp.sum(image * image))


def back(*refs, later):
    hops = refs[:4]
    before, scal = refs[4:6] if later else (None, None)
    high, low, image_out, scal_out, mine, theirs = refs[-6:]
    image, image_sq = step_image(hops, before, scal, image_out, scal_out)
    half = image.shape[0] // CORES
    stride = mine.shape[0] // half
    x2 = split2(image)
    for t in range(high.shape[1] // WIDE):
        p = rows_product(x2, high, low, pl.ds(t * WIDE, WIDE))
        store_pieces(mine, theirs, p, t, stride)
    extra = jnp.broadcast_to(image_sq, (half, LANES))
    mine[pl.ds(stride - 1, half, stride=stride), :] = extra
    theirs[pl.ds(stride - 1, half, stride=stride), :] = extra


def last_image(h0, h1, h2, h3, before, scal, image_out, scal_out, squares):
    _, image_sq = step_image((h0, h1, h2, h3), before, scal, image_out, scal_out)
    squares[...] = jnp.broadcast_to(image_sq, squares.shape)


def step_size(image_sq, scal):
    return scal[0:1, :] / (image_sq + ridge * scal[2:3, :])


def reduce_pieces(*refs, rows, scalars):
    if scalars:
        got, scal, out, size = refs
    else:
        got, out = refs
    count = out.shape[0] // rows
    stride = got.shape[0] // count
    terms = [got[i * stride : (i + 1) * stride, :] for i in range(count)]
    while len(terms) > 1:
        terms = [terms[i] + terms[i + 1] for i in range(0, len(terms), 2)]
    total = terms[0]
    for i in range(count):
        out[i * rows : (i + 1) * rows, :] = total[:rows]
    if scalars:
        size[...] = jnp.broadcast_to(step_size(total[rows : rows + 1], scal), size.shape)


def forward(*refs, step):
    if step == 0:
        top, bottom, high, low, gradient, out = refs
        g = jnp.concatenate([top[...], bottom[...]], axis=0)
        cross = None
    else:
        if step == 1:
            top, bottom, size, scal, g_old, high, low, gradient, direction, out = refs
            d = g_old[...]
        else:
            top, bottom, size, scal, g_old, d_old, high, low, gradient, direction, out = refs
            d = g_old[...] + scal[1:2, :] * d_old[...]
        q = jnp.concatenate([top[...], bottom[...]], axis=0)
        direction[...] = d
        g = g_old[...] - size[0:1, :] * (q + ridge * d)
        cross = jnp.sum(g * d)
    gradient[...] = g
    n = out.shape[0] - TILE
    stride = g.shape[0] // n
    x2 = split2(
        jnp.concatenate([gradient[pl.ds(j, n, stride=stride), :] for j in range(stride)], axis=1)
    )
    for t in range(high.shape[1] // WIDE):
        at = pl.ds(t * WIDE, WIDE)
        out[0:n, at] = rows_product(x2, high, low, at)
    out[n : n + 1, :] = jnp.broadcast_to(jnp.sum(g * g), (1, out.shape[1]))
    rest = jnp.zeros((TILE - 1, out.shape[1]), F32)
    out[n + 1 :, :] = rest if cross is None else rest + cross


def prepare(core, scal, size0, size1, d0, d1, g2, i0, i1, i2, targets, readout, direction, residual, image, sums):
    own = core[0, 0] == 0
    n = targets.shape[0]
    stride = d0.shape[0] // n
    s0, s1 = size0[0:1, :], size1[0:1, :]
    for value, out in (
        (s0 * d0[...] + s1 * d1[...], readout),
        (g2[...] + scal[1:2, :] * d1[...], direction),
    ):
        sums[...] = value
        for j in range(stride):
            out[:, pl.ds(j * LANES, LANES)] = own_half_first(
                sums[pl.ds(j, n, stride=stride), :], own
            )
    r = targets[...] - s0[:, :1] * i0[...] - s1[:, :1] * i1[...]
    residual[...] = own_half_first(r, own)
    image[...] = own_half_first(i2[...], own)


def finish(got, other, scal, readout_part, direction, residual_part, image, readout, residual):
    image_sq = jnp.sum(got[...] + other[...], axis=0, keepdims=True)
    size = step_size(image_sq, scal)[:, :1]
    readout[...] = readout_part[...] + size * direction[...]
    residual[...] = residual_part[...] - size * image[...]


def shards(states, targets):
    samples, units = states.shape
    outputs = targets.shape[1]
    samp_count = lax.axis_size("samp")
    unit_count = lax.axis_size("unit")
    chips = samp_count // CORES
    half = outputs // CORES
    rows = units // LANES
    core = jnp.full((1, 1), lax.axis_index("samp") % CORES, jnp.int32)

    swap_cores = [(i, i ^ 1) for i in range(samp_count)]
    groups = [[chip * CORES + c for chip in range(chips)] for c in range(CORES)]

    def swap(x):
        return lax.ppermute(x, "samp", swap_cores)

    def exchange(x):
        n = x.shape[0]
        x = x.reshape(n, 1, LANES)
        x = lax.all_to_all(x, "samp", 0, 0, axis_index_groups=groups, tiled=True)
        return x.reshape(n, LANES)

    def unit_terms(x):
        hops = [
            lax.ppermute(x, "unit", [(i, (i + d) % unit_count) for i in range(unit_count)])
            for d in range(1, unit_count)
        ]
        return [x] + hops

    vector = shape(TILE, LANES)
    image_shape = shape(outputs, samples)
    whole = shape(outputs * rows, LANES)
    partial = shape(outputs + TILE, samples)
    flops = 2 * 4 * samples * units * outputs

    smem = pl.BlockSpec(memory_space=pltpu.SMEM)
    high, low, turned, mine, theirs = call(
        first,
        [shape(samples, units, dtype=BF16)] * 2 + [image_shape] + [shape(half * rows, LANES)] * 2,
        core,
        pltpu.with_memory_space_constraint(states, pltpu.HBM),
        pltpu.with_memory_space_constraint(targets.T, pltpu.HBM),
        specs=[smem, HBM, HBM],
        scratch=[
            pltpu.VMEM((units // WIDE, samples, WIDE), F32),
            pltpu.VMEM((outputs, samples), F32),
            pltpu.SemaphoreType.DMA((units // WIDE + 1,)),
        ],
        limit=32,
        flops=flops,
    )
    high, low = here(high), here(low)
    high_turned, low_turned = call(
        turn_states, [shape(units, samples, dtype=BF16)] * 2, high, low, flops=flops
    )
    high_turned, low_turned = here(high_turned), here(low_turned)
    got = exchange(mine + swap(theirs))
    spread = call(reduce_pieces, shape(half * rows, LANES), got, rows=rows, scalars=False)

    gradients, directions, images, sizes = [], [], [], []
    scal = size = None
    for step in range(ITERS):
        top = exchange(spread)
        bottom = swap(top)
        if step == 0:
            g, out = call(
                forward,
                [whole, partial],
                top,
                bottom,
                high_turned,
                low_turned,
                step=0,
                flops=flops,
            )
        else:
            olds = [gradients[-1]] + ([directions[-1]] if step > 1 else [])
            g, d, out = call(
                forward,
                [whole, whole, partial],
                top,
                bottom,
                size,
                scal,
                *olds,
                high_turned,
                low_turned,
                step=step,
                flops=flops,
            )
            directions.append(d)
        gradients.append(g)
        hops = unit_terms(out)
        olds = [images[-1], scal] if step else []
        if step + 1 < ITERS:
            piece = shape(half * (rows + 1), LANES)
            image, scal, mine, theirs = call(
                back,
                [image_shape, vector, piece, piece],
                *hops,
                *olds,
                high,
                low,
                later=step > 0,
                flops=flops,
            )
            images.append(image)
            got = exchange(mine + swap(theirs))
            spread, size = call(
                reduce_pieces,
                [shape(half * rows, LANES), vector],
                got,
                scal,
                rows=rows,
                scalars=True,
            )
            sizes.append(size)
        else:
            image, scal, squares = call(
                last_image, [image_shape, vector, shape(half, LANES)], *hops, *olds
            )
            images.append(image)
            got = exchange(squares)
            other = swap(got)
    parts = call(
        prepare,
        [shape(outputs, units)] * 2 + [image_shape] * 2,
        core,
        scal,
        *sizes,
        *directions,
        gradients[-1],
        *images,
        turned,
        specs=[smem] + [VMEM] * 10,
        scratch=[pltpu.VMEM((outputs * rows, LANES), F32)],
        flops=flops,
    )
    readout, residual = call(
        finish, [shape(outputs, units), image_shape], got, other, scal, *parts
    )
    return readout.T, residual.T


def solution(mesh):
    return jax.shard_map(
        shards,
        mesh=mesh,
        in_specs=(P("samp", "unit"), P("samp", None)),
        out_specs=(P("unit", None), P("samp", None)),
        check_vma=False,
    )
```

```python
import functools

import jax
import jax.numpy as jnp
from jax import lax
from jax.experimental import pallas as pl
from jax.experimental.pallas import tpu as pltpu
from jax.sharding import PartitionSpec as P

ITERS = 3
ridge = 0.5
CORES, LANES, TILE = 2, 128, 8
WIDE = 256
MIB = 1 << 20
F32, BF16 = jnp.float32, jnp.bfloat16
VMEM = pl.BlockSpec(memory_space=pltpu.VMEM)
HBM = pl.BlockSpec(memory_space=pl.ANY)


def shape(*dims, dtype=F32):
    return jax.ShapeDtypeStruct(dims, dtype)


def here(x):
    return pltpu.with_memory_space_constraint(x, pltpu.VMEM)


def call(kernel, out_shape, *args, scratch=(), limit=24, specs=None, flops=0, **static):
    return pl.pallas_call(
        functools.partial(kernel, **static),
        in_specs=specs or [VMEM] * len(args),
        out_specs=jax.tree.map(lambda _: VMEM, out_shape),
        out_shape=out_shape,
        scratch_shapes=list(scratch),
        compiler_params=pltpu.CompilerParams(vmem_limit_bytes=limit * MIB),
        cost_estimate=pl.CostEstimate(flops=flops, bytes_accessed=MIB, transcendentals=0),
        name=kernel.__name__,
    )(*args)


def split2(x):
    high = x.astype(BF16)
    return jnp.concatenate([high, (x - high.astype(F32)).astype(BF16)], axis=0)


def dot(a, b, ca, cb):
    return lax.dot_general(a, b, (((ca,), (cb,)), ((), ())), preferred_element_type=F32)


def fold(p):
    n = p.shape[0] // 2
    return p[n:] + p[:n]


def rows_product(x, high, low, at):
    x2 = split2(x) if x.dtype == F32 else x
    return fold(dot(x2, low[:, at], 1, 0) + dot(x2, high[:, at], 1, 0))


def row(x):
    return jnp.broadcast_to(x, (1, LANES))


def store_pieces(mine, theirs, value, at, stride):
    half = value.shape[0] // CORES
    for i in range(WIDE // LANES):
        part = value[:, i * LANES : (i + 1) * LANES]
        j = at * (WIDE // LANES) + i
        mine[pl.ds(j, half, stride=stride), :] = part[:half]
        theirs[pl.ds(j, half, stride=stride), :] = part[half:]


def own_half_first(x, own):
    half = x.shape[0] // CORES
    top, bottom = x[:half], x[half:]
    return jnp.concatenate(
        [jnp.where(own, top, bottom), jnp.where(own, bottom, top)], axis=0
    )


def first(core, states, targets, high, low, turned, mine, theirs, buf, target_buf, sems):
    steps = buf.shape[0]
    fetch = pltpu.make_async_copy(targets, target_buf, sems.at[steps])
    fetch.start()
    copies = [
        pltpu.make_async_copy(
            states.at[:, pl.ds(t * WIDE, WIDE)], buf.at[t], sems.at[t]
        )
        for t in range(steps)
    ]
    for c in copies:
        c.start()
    fetch.wait()
    x = own_half_first(target_buf[...], core[0, 0] == 0)
    turned[...] = x
    x2 = split2(x)
    half = x.shape[0] // CORES
    for t in range(steps):
        copies[t].wait()
        s = buf[t]
        h = s.astype(BF16)
        l = (s - h.astype(F32)).astype(BF16)
        high[:, pl.ds(t * WIDE, WIDE)] = h
        low[:, pl.ds(t * WIDE, WIDE)] = l
        p = fold(dot(x2, l, 1, 0) + dot(x2, h, 1, 0))
        store_pieces(mine, theirs, p, t, mine.shape[0] // half)


def turn_states(x, turned):
    turned[...] = x[...].T


def combine(a, ra, b, rb):
    n = b.shape[0]
    image = jnp.concatenate([a[:n, :] + ra[:n, :], b[...] + rb[...]], axis=1)
    return image, a[n : n + TILE, :LANES] + ra[n : n + TILE, :LANES]


def step_image(hops, before, scal, image_out, scal_out):
    image, tail = combine(*hops)
    gamma = tail[0:1]
    if before is None:
        beta = jnp.zeros_like(gamma)
        square = gamma
    else:
        beta = gamma / scal[0:1, :]
        square = gamma + beta * (2.0 * tail[1:2] + beta * scal[2:3, :])
        image = image + beta[:, :1] * before[...]
    image_out[...] = image
    scal_out[0:1, :] = gamma
    scal_out[1:2, :] = beta
    scal_out[2:3, :] = square
    scal_out[3:, :] = jnp.zeros((TILE - 3, LANES), F32)
    return image, row(jnp.sum(image * image))


def back(*refs, later):
    hops = refs[:4]
    before, scal = refs[4:6] if later else (None, None)
    high, low, image_out, scal_out, mine, theirs = refs[-6:]
    image, image_sq = step_image(hops, before, scal, image_out, scal_out)
    half = image.shape[0] // CORES
    stride = mine.shape[0] // half
    x2 = split2(image)
    for t in range(high.shape[1] // WIDE):
        p = rows_product(x2, high, low, pl.ds(t * WIDE, WIDE))
        store_pieces(mine, theirs, p, t, stride)
    extra = jnp.broadcast_to(image_sq, (half, LANES))
    mine[pl.ds(stride - 1, half, stride=stride), :] = extra
    theirs[pl.ds(stride - 1, half, stride=stride), :] = extra


def last_image(h0, h1, h2, h3, before, scal, image_out, scal_out, squares):
    _, image_sq = step_image((h0, h1, h2, h3), before, scal, image_out, scal_out)
    squares[...] = jnp.broadcast_to(image_sq, squares.shape)


def step_size(image_sq, scal):
    return scal[0:1, :] / (image_sq + ridge * scal[2:3, :])


def reduce_pieces(*refs, rows, scalars):
    if scalars:
        got, scal, out, size = refs
    else:
        got, out = refs
    count = out.shape[0] // rows
    stride = got.shape[0] // count
    terms = [got[i * stride : (i + 1) * stride, :] for i in range(count)]
    while len(terms) > 1:
        terms = [terms[i] + terms[i + 1] for i in range(0, len(terms), 2)]
    total = terms[0]
    for i in range(count):
        out[i * rows : (i + 1) * rows, :] = total[:rows]
    if scalars:
        size[...] = jnp.broadcast_to(step_size(total[rows : rows + 1], scal), size.shape)


def forward(*refs, step):
    if step == 0:
        top, bottom, high, low, gradient, a, b = refs
        g = jnp.concatenate([top[...], bottom[...]], axis=0)
        cross = None
    else:
        if step == 1:
            top, bottom, size, scal, g_old, high, low, gradient, direction, a, b = refs
            d = g_old[...]
        else:
            top, bottom, size, scal, g_old, d_old, high, low, gradient, direction, a, b = refs
            d = g_old[...] + scal[1:2, :] * d_old[...]
        q = jnp.concatenate([top[...], bottom[...]], axis=0)
        direction[...] = d
        g = g_old[...] - size[0:1, :] * (q + ridge * d)
        cross = jnp.sum(g * d)
    gradient[...] = g
    n = b.shape[0]
    stride = g.shape[0] // n
    x2 = split2(
        jnp.concatenate([gradient[pl.ds(j, n, stride=stride), :] for j in range(stride)], axis=1)
    )
    steps = high.shape[1] // WIDE
    for t in range(steps):
        p = rows_product(x2, high, low, pl.ds(t * WIDE, WIDE))
        out, k = (a, t) if t < steps // 2 else (b, t - steps // 2)
        out[0:n, k * WIDE : (k + 1) * WIDE] = p
    a[n : n + 1, :] = jnp.broadcast_to(jnp.sum(g * g), (1, a.shape[1]))
    rest = jnp.zeros((TILE - 1, a.shape[1]), F32)
    a[n + 1 :, :] = rest if cross is None else rest + cross


def prepare(core, scal, size0, size1, d0, d1, g2, i0, i1, i2, targets, readout, direction, residual, image, sums):
    own = core[0, 0] == 0
    n = targets.shape[0]
    stride = d0.shape[0] // n
    s0, s1 = size0[0:1, :], size1[0:1, :]
    for value, out in (
        (s0 * d0[...] + s1 * d1[...], readout),
        (g2[...] + scal[1:2, :] * d1[...], direction),
    ):
        sums[...] = value
        for j in range(stride):
            out[:, pl.ds(j * LANES, LANES)] = own_half_first(
                sums[pl.ds(j, n, stride=stride), :], own
            )
    r = targets[...] - s0[:, :1] * i0[...] - s1[:, :1] * i1[...]
    residual[...] = own_half_first(r, own)
    image[...] = own_half_first(i2[...], own)


def finish(got, other, scal, readout_part, direction, residual_part, image, readout, residual):
    image_sq = jnp.sum(got[...] + other[...], axis=0, keepdims=True)
    size = step_size(image_sq, scal)[:, :1]
    readout[...] = readout_part[...] + size * direction[...]
    residual[...] = residual_part[...] - size * image[...]


def shards(states, targets):
    samples, units = states.shape
    outputs = targets.shape[1]
    samp_count = lax.axis_size("samp")
    unit_count = lax.axis_size("unit")
    chips = samp_count // CORES
    half = outputs // CORES
    rows = units // LANES
    core = jnp.full((1, 1), lax.axis_index("samp") % CORES, jnp.int32)

    swap_cores = [(i, i ^ 1) for i in range(samp_count)]
    groups = [[chip * CORES + c for chip in range(chips)] for c in range(CORES)]

    def swap(x):
        return lax.ppermute(x, "samp", swap_cores)

    def exchange(x):
        n = x.shape[0]
        parts = (half, rows, LANES) if n == half * rows else (half, 1, n // half * LANES)
        x = x.reshape(parts)
        x = lax.all_to_all(x, "samp", 0, 0, axis_index_groups=groups, tiled=True)
        return x.reshape(n, LANES)

    def unit_hop(x, mask):
        return lax.ppermute(x, "unit", [(i, i ^ mask) for i in range(unit_count)])

    def unit_terms(a, b):
        a, b = a + unit_hop(a, 1), b + unit_hop(b, 3)
        return a, unit_hop(a, 3), b, unit_hop(b, 1)

    vector = shape(TILE, LANES)
    image_shape = shape(outputs, samples)
    whole = shape(outputs * rows, LANES)
    partial = [shape(outputs + TILE, samples // 2), shape(outputs, samples // 2)]
    flops = 2 * 4 * samples * units * outputs

    smem = pl.BlockSpec(memory_space=pltpu.SMEM)
    high, low, turned, mine, theirs = call(
        first,
        [shape(samples, units, dtype=BF16)] * 2 + [image_shape] + [shape(half * rows, LANES)] * 2,
        core,
        pltpu.with_memory_space_constraint(states, pltpu.HBM),
        pltpu.with_memory_space_constraint(targets.T, pltpu.HBM),
        specs=[smem, HBM, HBM],
        scratch=[
            pltpu.VMEM((units // WIDE, samples, WIDE), F32),
            pltpu.VMEM((outputs, samples), F32),
            pltpu.SemaphoreType.DMA((units // WIDE + 1,)),
        ],
        limit=32,
        flops=flops,
    )
    high, low = here(high), here(low)
    high_turned, low_turned = [
        here(call(turn_states, shape(units, samples, dtype=BF16), x, flops=flops))
        for x in (high, low)
    ]
    got = exchange(mine + swap(theirs))
    spread = call(reduce_pieces, shape(half * rows, LANES), got, rows=rows, scalars=False)

    gradients, directions, images, sizes = [], [], [], []
    scal = size = None
    for step in range(ITERS):
        top = exchange(spread)
        bottom = swap(top)
        if step == 0:
            g, *terms = call(
                forward,
                [whole] + partial,
                top,
                bottom,
                high_turned,
                low_turned,
                step=0,
                flops=flops,
            )
        else:
            olds = [gradients[-1]] + ([directions[-1]] if step > 1 else [])
            g, d, *terms = call(
                forward,
                [whole, whole] + partial,
                top,
                bottom,
                size,
                scal,
                *olds,
                high_turned,
                low_turned,
                step=step,
                flops=flops,
            )
            directions.append(d)
        gradients.append(g)
        hops = unit_terms(*terms)
        olds = [images[-1], scal] if step else []
        if step + 1 < ITERS:
            piece = shape(half * (rows + 1), LANES)
            image, scal, mine, theirs = call(
                back,
                [image_shape, vector, piece, piece],
                *hops,
                *olds,
                high,
                low,
                later=step > 0,
                flops=flops,
            )
            images.append(image)
            got = exchange(mine + swap(theirs))
            spread, size = call(
                reduce_pieces,
                [shape(half * rows, LANES), vector],
                got,
                scal,
                rows=rows,
                scalars=True,
            )
            sizes.append(size)
        else:
            image, scal, squares = call(
                last_image, [image_shape, vector, shape(half, LANES)], *hops, *olds
            )
            images.append(image)
            got = exchange(squares)
            other = swap(got)
    parts = call(
        prepare,
        [shape(outputs, units)] * 2 + [image_shape] * 2,
        core,
        scal,
        *sizes,
        *directions,
        gradients[-1],
        *images,
        turned,
        specs=[smem] + [VMEM] * 10,
        scratch=[pltpu.VMEM((outputs * rows, LANES), F32)],
        flops=flops,
    )
    readout, residual = call(
        finish, [shape(outputs, units), image_shape], got, other, scal, *parts
    )
    return readout.T, residual.T


def solution(mesh):
    return jax.shard_map(
        shards,
        mesh=mesh,
        in_specs=(P("samp", "unit"), P("samp", None)),
        out_specs=(P("unit", None), P("samp", None)),
        check_vma=False,
    )
```

```python
import functools

import jax
import jax.numpy as jnp
from jax import lax
from jax.experimental import pallas as pl
from jax.experimental.pallas import tpu as pltpu
from jax.sharding import PartitionSpec as P

ITERS = 3
ridge = 0.5
CORES, LANES, TILE = 2, 128, 8
WIDE, FETCH = 256, 512
MIB = 1 << 20
F32, BF16 = jnp.float32, jnp.bfloat16
VMEM = pl.BlockSpec(memory_space=pltpu.VMEM)
HBM = pl.BlockSpec(memory_space=pl.ANY)


def shape(*dims, dtype=F32):
    return jax.ShapeDtypeStruct(dims, dtype)


def here(x):
    return pltpu.with_memory_space_constraint(x, pltpu.VMEM)


def call(kernel, out_shape, *args, scratch=(), limit=24, specs=None, flops=0, **static):
    return pl.pallas_call(
        functools.partial(kernel, **static),
        in_specs=specs or [VMEM] * len(args),
        out_specs=jax.tree.map(lambda _: VMEM, out_shape),
        out_shape=out_shape,
        scratch_shapes=list(scratch),
        compiler_params=pltpu.CompilerParams(vmem_limit_bytes=limit * MIB),
        cost_estimate=pl.CostEstimate(flops=flops, bytes_accessed=MIB, transcendentals=0),
        name=kernel.__name__,
    )(*args)


def split2(x):
    high = x.astype(BF16)
    return jnp.concatenate([high, (x - high.astype(F32)).astype(BF16)], axis=0)


def dot(a, b, ca, cb):
    return lax.dot_general(a, b, (((ca,), (cb,)), ((), ())), preferred_element_type=F32)


def fold(p):
    n = p.shape[0] // 2
    return p[n:] + p[:n]


def rows_product(x, high, low, at):
    x2 = split2(x) if x.dtype == F32 else x
    return fold(dot(x2, low[:, at], 1, 0) + dot(x2, high[:, at], 1, 0))


def row(x):
    return jnp.broadcast_to(x, (1, LANES))


def store_pieces(mine, theirs, value, at, stride):
    half = value.shape[0] // CORES
    for i in range(WIDE // LANES):
        part = value[:, i * LANES : (i + 1) * LANES]
        j = at * (WIDE // LANES) + i
        mine[pl.ds(j, half, stride=stride), :] = part[:half]
        theirs[pl.ds(j, half, stride=stride), :] = part[half:]


def own_half_first(x, own):
    half = x.shape[0] // CORES
    top, bottom = x[:half], x[half:]
    return jnp.concatenate(
        [jnp.where(own, top, bottom), jnp.where(own, bottom, top)], axis=0
    )


def first(core, states, targets, high, low, turned, mine, theirs, buf, target_buf, sems):
    steps = buf.shape[0]
    fetch = pltpu.make_async_copy(targets, target_buf, sems.at[steps])
    fetch.start()
    copies = [
        pltpu.make_async_copy(
            states.at[:, pl.ds(t * FETCH, FETCH)], buf.at[t], sems.at[t]
        )
        for t in range(steps)
    ]
    for c in copies:
        c.start()
    fetch.wait()
    x = own_half_first(target_buf[...], core[0, 0] == 0)
    turned[...] = x
    x2 = split2(x)
    half = x.shape[0] // CORES
    for t in range(steps):
        copies[t].wait()
        s = buf[t]
        h = s.astype(BF16)
        l = (s - h.astype(F32)).astype(BF16)
        high[:, pl.ds(t * FETCH, FETCH)] = h
        low[:, pl.ds(t * FETCH, FETCH)] = l
        p = fold(dot(x2, l, 1, 0) + dot(x2, h, 1, 0))
        for i in range(FETCH // WIDE):
            part = p[:, i * WIDE : (i + 1) * WIDE]
            store_pieces(mine, theirs, part, t * (FETCH // WIDE) + i, mine.shape[0] // half)


def turn_states(x, turned, token):
    turned[...] = x[...].T
    token[...] = jnp.zeros(token.shape, F32)


def combine(a, ra, b, rb):
    n = b.shape[0]
    image = jnp.concatenate([a[:n, :] + ra[:n, :], b[...] + rb[...]], axis=1)
    return image, a[n : n + TILE, :LANES] + ra[n : n + TILE, :LANES]


def step_image(hops, before, scal, image_out, scal_out):
    image, tail = combine(*hops)
    gamma = tail[0:1]
    if before is None:
        beta = jnp.zeros_like(gamma)
        square = gamma
    else:
        beta = gamma / scal[0:1, :]
        square = gamma + beta * (2.0 * tail[1:2] + beta * scal[2:3, :])
        image = image + beta[:, :1] * before[...]
    image_out[...] = image
    scal_out[0:1, :] = gamma
    scal_out[1:2, :] = beta
    scal_out[2:3, :] = square
    scal_out[3:, :] = jnp.zeros((TILE - 3, LANES), F32)
    return image, row(jnp.sum(image * image))


def back(*refs, later):
    hops = refs[:4]
    before, scal = refs[4:6] if later else (None, None)
    high, low, image_out, scal_out, mine, theirs = refs[-6:]
    image, image_sq = step_image(hops, before, scal, image_out, scal_out)
    half = image.shape[0] // CORES
    stride = mine.shape[0] // half
    x2 = split2(image)
    for t in range(high.shape[1] // WIDE):
        p = rows_product(x2, high, low, pl.ds(t * WIDE, WIDE))
        store_pieces(mine, theirs, p, t, stride)
    extra = jnp.broadcast_to(image_sq, (half, LANES))
    mine[pl.ds(stride - 1, half, stride=stride), :] = extra
    theirs[pl.ds(stride - 1, half, stride=stride), :] = extra


def last_image(h0, h1, h2, h3, before, scal, image_out, scal_out, squares):
    _, image_sq = step_image((h0, h1, h2, h3), before, scal, image_out, scal_out)
    squares[...] = jnp.broadcast_to(image_sq, squares.shape)


def step_size(image_sq, scal):
    return scal[0:1, :] / (image_sq + ridge * scal[2:3, :])


def sum_pieces(got, out, rows):
    count = out.shape[0] // rows
    stride = got.shape[0] // count
    terms = [got[i * stride : (i + 1) * stride, :] for i in range(count)]
    while len(terms) > 1:
        terms = [terms[i] + terms[i + 1] for i in range(0, len(terms), 2)]
    total = terms[0]
    for i in range(count):
        out[i * rows : (i + 1) * rows, :] = total[:rows]
    return total


def add_pieces(a, b, token, out):
    out[...] = a[...] + b[...]


def reduce_first(got, out, rows):
    sum_pieces(got, out, rows)


def reduce_pieces(got, scal, out, size, rows):
    total = sum_pieces(got, out, rows)
    size[...] = jnp.broadcast_to(step_size(total[rows : rows + 1], scal), size.shape)


def forward(*refs, step):
    if step == 0:
        top, bottom, high, low, gradient, a, b = refs
        g = jnp.concatenate([top[...], bottom[...]], axis=0)
        cross = None
    else:
        if step == 1:
            top, bottom, size, scal, g_old, high, low, gradient, direction, a, b = refs
            d = g_old[...]
        else:
            top, bottom, size, scal, g_old, d_old, high, low, gradient, direction, a, b = refs
            d = g_old[...] + scal[1:2, :] * d_old[...]
        q = jnp.concatenate([top[...], bottom[...]], axis=0)
        direction[...] = d
        g = g_old[...] - size[0:1, :] * (q + ridge * d)
        cross = jnp.sum(g * d)
    gradient[...] = g
    n = b.shape[0]
    stride = g.shape[0] // n
    x2 = split2(
        jnp.concatenate([gradient[pl.ds(j, n, stride=stride), :] for j in range(stride)], axis=1)
    )
    steps = high.shape[1] // WIDE
    for t in range(steps):
        p = rows_product(x2, high, low, pl.ds(t * WIDE, WIDE))
        out, k = (a, t) if t < steps // 2 else (b, t - steps // 2)
        out[0:n, k * WIDE : (k + 1) * WIDE] = p
    a[n : n + 1, :] = jnp.broadcast_to(jnp.sum(g * g), (1, a.shape[1]))
    rest = jnp.zeros((TILE - 1, a.shape[1]), F32)
    a[n + 1 :, :] = rest if cross is None else rest + cross


def prepare(core, scal, size0, size1, d0, d1, g2, i0, i1, i2, targets, readout, direction, residual, image, sums):
    own = core[0, 0] == 0
    n = targets.shape[0]
    stride = d0.shape[0] // n
    s0, s1 = size0[0:1, :], size1[0:1, :]
    for value, out in (
        (s0 * d0[...] + s1 * d1[...], readout),
        (g2[...] + scal[1:2, :] * d1[...], direction),
    ):
        sums[...] = value
        for j in range(stride):
            out[:, pl.ds(j * LANES, LANES)] = own_half_first(
                sums[pl.ds(j, n, stride=stride), :], own
            )
    r = targets[...] - s0[:, :1] * i0[...] - s1[:, :1] * i1[...]
    residual[...] = own_half_first(r, own)
    image[...] = own_half_first(i2[...], own)


def finish(got, other, scal, readout_part, direction, residual_part, image, readout, residual):
    image_sq = jnp.sum(got[...] + other[...], axis=0, keepdims=True)
    size = step_size(image_sq, scal)[:, :1]
    readout[...] = readout_part[...] + size * direction[...]
    residual[...] = residual_part[...] - size * image[...]


def shards(states, targets):
    samples, units = states.shape
    outputs = targets.shape[1]
    samp_count = lax.axis_size("samp")
    unit_count = lax.axis_size("unit")
    chips = samp_count // CORES
    half = outputs // CORES
    rows = units // LANES
    core = jnp.full((1, 1), lax.axis_index("samp") % CORES, jnp.int32)

    swap_cores = [(i, i ^ 1) for i in range(samp_count)]
    groups = [[chip * CORES + c for chip in range(chips)] for c in range(CORES)]

    def swap(x):
        return lax.ppermute(x, "samp", swap_cores)

    def exchange(x):
        n = x.shape[0]
        parts = (half, rows, LANES) if n == half * rows else (half, 1, n // half * LANES)
        x = x.reshape(parts)
        x = lax.all_to_all(x, "samp", 0, 0, axis_index_groups=groups, tiled=True)
        return x.reshape(n, LANES)

    def unit_hop(x, mask):
        return lax.ppermute(x, "unit", [(i, i ^ mask) for i in range(unit_count)])

    def unit_terms(a, b):
        a, b = a + unit_hop(a, 1), b + unit_hop(b, 3)
        return a, unit_hop(a, 3), b, unit_hop(b, 1)

    vector = shape(TILE, LANES)
    image_shape = shape(outputs, samples)
    whole = shape(outputs * rows, LANES)
    partial = [shape(outputs + TILE, samples // 2), shape(outputs, samples // 2)]
    flops = 2 * 4 * samples * units * outputs

    smem = pl.BlockSpec(memory_space=pltpu.SMEM)
    high, low, turned, mine, theirs = call(
        first,
        [shape(samples, units, dtype=BF16)] * 2 + [image_shape] + [shape(half * rows, LANES)] * 2,
        core,
        pltpu.with_memory_space_constraint(states, pltpu.HBM),
        pltpu.with_memory_space_constraint(targets.T, pltpu.HBM),
        specs=[smem, HBM, HBM],
        scratch=[
            pltpu.VMEM((units // FETCH, samples, FETCH), F32),
            pltpu.VMEM((outputs, samples), F32),
            pltpu.SemaphoreType.DMA((units // FETCH + 1,)),
        ],
        limit=32,
        flops=flops,
    )
    high, low = here(high), here(low)
    (high_turned, token), (low_turned, _) = [
        call(turn_states, [shape(units, samples, dtype=BF16), vector], x, flops=flops)
        for x in (high, low)
    ]
    high_turned, low_turned = here(high_turned), here(low_turned)
    pieces = call(add_pieces, shape(half * rows, LANES), mine, swap(theirs), token)
    got = exchange(pieces)
    spread = call(reduce_first, shape(half * rows, LANES), got, rows=rows)

    gradients, directions, images, sizes = [], [], [], []
    scal = size = None
    for step in range(ITERS):
        top = exchange(spread)
        bottom = swap(top)
        if step == 0:
            g, *terms = call(
                forward,
                [whole] + partial,
                top,
                bottom,
                high_turned,
                low_turned,
                step=0,
                flops=flops,
            )
        else:
            olds = [gradients[-1]] + ([directions[-1]] if step > 1 else [])
            g, d, *terms = call(
                forward,
                [whole, whole] + partial,
                top,
                bottom,
                size,
                scal,
                *olds,
                high_turned,
                low_turned,
                step=step,
                flops=flops,
            )
            directions.append(d)
        gradients.append(g)
        hops = unit_terms(*terms)
        olds = [images[-1], scal] if step else []
        if step + 1 < ITERS:
            piece = shape(half * (rows + 1), LANES)
            image, scal, mine, theirs = call(
                back,
                [image_shape, vector, piece, piece],
                *hops,
                *olds,
                high,
                low,
                later=step > 0,
                flops=flops,
            )
            images.append(image)
            got = exchange(mine + swap(theirs))
            spread, size = call(
                reduce_pieces,
                [shape(half * rows, LANES), vector],
                got,
                scal,
                rows=rows,
            )
            sizes.append(size)
        else:
            image, scal, squares = call(
                last_image, [image_shape, vector, shape(half, LANES)], *hops, *olds
            )
            images.append(image)
            got = exchange(squares)
            other = swap(got)
    parts = call(
        prepare,
        [shape(outputs, units)] * 2 + [image_shape] * 2,
        core,
        scal,
        *sizes,
        *directions,
        gradients[-1],
        *images,
        turned,
        specs=[smem] + [VMEM] * 10,
        scratch=[pltpu.VMEM((outputs * rows, LANES), F32)],
        flops=flops,
    )
    readout, residual = call(
        finish, [shape(outputs, units), image_shape], got, other, scal, *parts
    )
    return readout.T, residual.T


def solution(mesh):
    return jax.shard_map(
        shards,
        mesh=mesh,
        in_specs=(P("samp", "unit"), P("samp", None)),
        out_specs=(P("unit", None), P("samp", None)),
        check_vma=False,
    )
```

```python
import functools

import jax
import jax.numpy as jnp
from jax import lax
from jax.experimental import pallas as pl
from jax.experimental.pallas import tpu as pltpu
from jax.sharding import PartitionSpec as P

ITERS = 3
ridge = 0.5
CORES, BLOCK, LANES, TILE = 2, 8, 128, 8
WIDE, FETCH = 256, 512
MIB = 1 << 20
F32, BF16 = jnp.float32, jnp.bfloat16
VMEM = pl.BlockSpec(memory_space=pltpu.VMEM)
HBM = pl.BlockSpec(memory_space=pl.ANY)


def shape(*dims, dtype=F32):
    return jax.ShapeDtypeStruct(dims, dtype)


def here(x):
    return pltpu.with_memory_space_constraint(x, pltpu.VMEM)


def call(kernel, out_shape, *args, scratch=(), limit=24, specs=None, flops=0, **static):
    return pl.pallas_call(
        functools.partial(kernel, **static),
        in_specs=specs or [VMEM] * len(args),
        out_specs=jax.tree.map(lambda _: VMEM, out_shape),
        out_shape=out_shape,
        scratch_shapes=list(scratch),
        compiler_params=pltpu.CompilerParams(vmem_limit_bytes=limit * MIB),
        cost_estimate=pl.CostEstimate(flops=flops, bytes_accessed=MIB, transcendentals=0),
        name=kernel.__name__,
    )(*args)


def split2(x):
    high = x.astype(BF16)
    return jnp.concatenate([high, (x - high.astype(F32)).astype(BF16)], axis=0)


def dot(a, b, ca, cb):
    return lax.dot_general(a, b, (((ca,), (cb,)), ((), ())), preferred_element_type=F32)


def fold(p):
    n = p.shape[0] // 2
    return p[n:] + p[:n]


def rows_product(x, high, low, at):
    x2 = split2(x) if x.dtype == F32 else x
    return fold(dot(x2, low[:, at], 1, 0) + dot(x2, high[:, at], 1, 0))


def row(x):
    return jnp.broadcast_to(x, (1, LANES))


def store_pieces(mine, theirs, value, at, stride):
    half = value.shape[0] // CORES
    for i in range(WIDE // LANES):
        part = value[:, i * LANES : (i + 1) * LANES]
        j = at * (WIDE // LANES) + i
        mine[pl.ds(j, half, stride=stride), :] = part[:half]
        theirs[pl.ds(j, half, stride=stride), :] = part[half:]


def own_half_first(x, own):
    half = x.shape[0] // CORES
    top, bottom = x[:half], x[half:]
    return jnp.concatenate(
        [jnp.where(own, top, bottom), jnp.where(own, bottom, top)], axis=0
    )


def first(core, states, targets, high, low, turned, mine, theirs, buf, target_buf, sems):
    steps = buf.shape[0]
    fetch = pltpu.make_async_copy(targets, target_buf, sems.at[steps])
    fetch.start()
    copies = [
        pltpu.make_async_copy(
            states.at[:, pl.ds(t * FETCH, FETCH)], buf.at[t], sems.at[t]
        )
        for t in range(steps)
    ]
    for c in copies:
        c.start()
    fetch.wait()
    x = own_half_first(target_buf[...], core[0, 0] == 0)
    turned[...] = x
    x2 = split2(x)
    half = x.shape[0] // CORES
    for t in range(steps):
        copies[t].wait()
        s = buf[t]
        h = s.astype(BF16)
        l = (s - h.astype(F32)).astype(BF16)
        high[:, pl.ds(t * FETCH, FETCH)] = h
        low[:, pl.ds(t * FETCH, FETCH)] = l
        p = fold(dot(x2, l, 1, 0) + dot(x2, h, 1, 0))
        for i in range(FETCH // WIDE):
            part = p[:, i * WIDE : (i + 1) * WIDE]
            store_pieces(mine, theirs, part, t * (FETCH // WIDE) + i, mine.shape[0] // half)


def turn_states(x, turned, token):
    turned[...] = x[...].T
    token[...] = jnp.zeros(token.shape, F32)


def combine(a, ra, b, rb):
    n = b.shape[0]
    image = jnp.concatenate([a[:n, :] + ra[:n, :], b[...] + rb[...]], axis=1)
    return image, a[n : n + TILE, :LANES] + ra[n : n + TILE, :LANES]


def step_image(hops, before, scal, image_out, scal_out):
    image, tail = combine(*hops)
    gamma = tail[0:1]
    if before is None:
        beta = jnp.zeros_like(gamma)
        square = gamma
    else:
        beta = gamma / scal[0:1, :]
        square = gamma + beta * (2.0 * tail[1:2] + beta * scal[2:3, :])
        image = image + beta[:, :1] * before[...]
    image_out[...] = image
    scal_out[0:1, :] = gamma
    scal_out[1:2, :] = beta
    scal_out[2:3, :] = square
    scal_out[3:, :] = jnp.zeros((TILE - 3, LANES), F32)
    return image, row(jnp.sum(image * image))


def back(*refs, later):
    hops = refs[:4]
    before, scal = refs[4:6] if later else (None, None)
    high, low, image_out, scal_out, mine, theirs = refs[-6:]
    image, image_sq = step_image(hops, before, scal, image_out, scal_out)
    half = image.shape[0] // CORES
    stride = mine.shape[0] // half
    x2 = split2(image)
    for t in range(high.shape[1] // WIDE):
        p = rows_product(x2, high, low, pl.ds(t * WIDE, WIDE))
        store_pieces(mine, theirs, p, t, stride)
    extra = jnp.broadcast_to(image_sq, (half, LANES))
    for j in range(high.shape[1] // LANES, stride):
        mine[pl.ds(j, half, stride=stride), :] = extra
        theirs[pl.ds(j, half, stride=stride), :] = extra


def last_image(h0, h1, h2, h3, before, scal, token, image_out, scal_out, squares):
    _, image_sq = step_image((h0, h1, h2, h3), before, scal, image_out, scal_out)
    squares[...] = jnp.broadcast_to(image_sq, squares.shape)


def step_size(image_sq, scal):
    return scal[0:1, :] / (image_sq + ridge * scal[2:3, :])


def add_pieces(a, b, token, out):
    out[...] = a[...] + b[...]


def sum_pieces(got, out):
    n = out.shape[0]
    terms = [got[i * n : (i + 1) * n, :] for i in range(got.shape[0] // n)]
    while len(terms) > 1:
        terms = [terms[i] + terms[i + 1] for i in range(0, len(terms), 2)]
    out[...] = terms[0]


def sum_blocks(*refs, rows, copies):
    a, b, *rest = refs
    total = a[...] + b[...]
    out = rest[-2] if len(rest) == 3 else rest[-1]
    n = out.shape[0] // copies
    stride = total.shape[0] // (n // rows)
    for i in range(n // rows):
        part = total[i * stride : i * stride + rows]
        for k in range(copies):
            out[k * n + i * rows : k * n + (i + 1) * rows, :] = part
    if len(rest) == 3:
        scal, _, size = rest
        size[...] = jnp.broadcast_to(step_size(total[rows : rows + 1], scal), size.shape)


def forward(*refs, step):
    if step == 0:
        top, bottom, high, low, gradient, a, b = refs
        g = jnp.concatenate([top[...], bottom[...]], axis=0)
        cross = None
    else:
        if step == 1:
            top, bottom, size, scal, g_old, high, low, gradient, direction, a, b = refs
            d = g_old[...]
        else:
            top, bottom, size, scal, g_old, d_old, high, low, gradient, direction, a, b = refs
            d = g_old[...] + scal[1:2, :] * d_old[...]
        q = jnp.concatenate([top[...], bottom[...]], axis=0)
        direction[...] = d
        g = g_old[...] - size[0:1, :] * (q + ridge * d)
        cross = jnp.sum(g * d)
    gradient[...] = g
    n = b.shape[0]
    stride = g.shape[0] // n
    x2 = split2(
        jnp.concatenate([gradient[pl.ds(j, n, stride=stride), :] for j in range(stride)], axis=1)
    )
    steps = high.shape[1] // WIDE
    for t in range(steps):
        p = rows_product(x2, high, low, pl.ds(t * WIDE, WIDE))
        out, k = (a, t) if t < steps // 2 else (b, t - steps // 2)
        out[0:n, k * WIDE : (k + 1) * WIDE] = p
    a[n : n + 1, :] = jnp.broadcast_to(jnp.sum(g * g), (1, a.shape[1]))
    rest = jnp.zeros((TILE - 1, a.shape[1]), F32)
    a[n + 1 :, :] = rest if cross is None else rest + cross


def prepare(core, size0, size1, d0, d1, g2, i0, i1, targets, readout, before, gradient, residual, token, sums):
    own = core[0, 0] == 0
    n = targets.shape[0]
    stride = d0.shape[0] // n
    s0, s1 = size0[0:1, :], size1[0:1, :]
    sums[...] = s0 * d0[...] + s1 * d1[...]
    for source, out in ((sums, readout), (d1, before), (g2, gradient)):
        for j in range(stride):
            out[:, pl.ds(j * LANES, LANES)] = own_half_first(
                source[pl.ds(j, n, stride=stride), :], own
            )
    r = targets[...] - s0[:, :1] * i0[...] - s1[:, :1] * i1[...]
    residual[...] = own_half_first(r, own)
    token[...] = jnp.zeros(token.shape, F32)


def finish(core, squares, others, scal, image, readout_part, before, gradient, residual_part, readout, residual):
    image_sq = jnp.sum(squares[...] + others[...], axis=0, keepdims=True)
    size = step_size(image_sq, scal)[:, :1]
    beta = scal[1:2, :1]
    readout[...] = readout_part[...] + size * (gradient[...] + beta * before[...])
    last = own_half_first(image[...], core[0, 0] == 0)
    residual[...] = residual_part[...] - size * last


def shards(states, targets):
    samples, units = states.shape
    outputs = targets.shape[1]
    samp_count = lax.axis_size("samp")
    unit_count = lax.axis_size("unit")
    chips = samp_count // CORES
    half = outputs // CORES
    rows = units // LANES
    vector = shape(TILE, LANES)
    core = jnp.full((1, 1), lax.axis_index("samp") % CORES, jnp.int32)

    swap_cores = [(i, i ^ 1) for i in range(samp_count)]
    blocks = chips // BLOCK
    assert blocks == 4
    groups = [
        [(block * BLOCK + chip) * CORES + c for chip in range(BLOCK)]
        for block in range(blocks)
        for c in range(CORES)
    ]

    def swap(x):
        return lax.ppermute(x, "samp", swap_cores)

    def exchange(x):
        n = x.shape[0]
        x = x.reshape(BLOCK, n // BLOCK, LANES)
        x = lax.all_to_all(x, "samp", 0, 0, axis_index_groups=groups, tiled=True)
        return x.reshape(n, LANES)

    def block_hop(x, mask):
        step = BLOCK * CORES
        return lax.ppermute(x, "samp", [(i, i ^ (mask * step)) for i in range(samp_count)])

    def block_terms(x):
        x = x + block_hop(x, 1)
        return x, block_hop(x, 3)

    def sum_samples(pieces, scal):
        n = pieces.shape[0] // BLOCK
        terms = block_terms(call(sum_pieces, shape(n, LANES), exchange(pieces)))
        outs = [shape(half * rows, LANES)] + ([] if scal is None else [vector])
        scals = [] if scal is None else [scal]
        outs = call(sum_blocks, outs, *terms, *scals, rows=rows, copies=BLOCK)
        return outs[0], outs[-1]

    def unit_hop(x, mask):
        return lax.ppermute(x, "unit", [(i, i ^ mask) for i in range(unit_count)])

    def unit_terms(a, b):
        a, b = a + unit_hop(a, 1), b + unit_hop(b, 3)
        return a, unit_hop(a, 3), b, unit_hop(b, 1)

    image_shape = shape(outputs, samples)
    whole = shape(outputs * rows, LANES)
    partial = [shape(outputs + TILE, samples // 2), shape(outputs, samples // 2)]
    flops = 2 * 4 * samples * units * outputs

    smem = pl.BlockSpec(memory_space=pltpu.SMEM)
    high, low, turned, mine, theirs = call(
        first,
        [shape(samples, units, dtype=BF16)] * 2 + [image_shape] + [shape(half * rows, LANES)] * 2,
        core,
        pltpu.with_memory_space_constraint(states, pltpu.HBM),
        pltpu.with_memory_space_constraint(targets.T, pltpu.HBM),
        specs=[smem, HBM, HBM],
        scratch=[
            pltpu.VMEM((units // FETCH, samples, FETCH), F32),
            pltpu.VMEM((outputs, samples), F32),
            pltpu.SemaphoreType.DMA((units // FETCH + 1,)),
        ],
        limit=32,
        flops=flops,
    )
    high, low = here(high), here(low)
    (high_turned, token), (low_turned, _) = [
        call(turn_states, [shape(units, samples, dtype=BF16), vector], x, flops=flops)
        for x in (high, low)
    ]
    high_turned, low_turned = here(high_turned), here(low_turned)
    pieces = call(add_pieces, shape(half * rows, LANES), mine, swap(theirs), token)
    spread, _ = sum_samples(pieces, None)

    gradients, directions, images, sizes = [], [], [], []
    scal = size = None
    for step in range(ITERS):
        top = exchange(spread)
        bottom = swap(top)
        if step == 0:
            g, *terms = call(
                forward,
                [whole] + partial,
                top,
                bottom,
                high_turned,
                low_turned,
                step=0,
                flops=flops,
            )
        else:
            olds = [gradients[-1]] + ([directions[-1]] if step > 1 else [])
            g, d, *terms = call(
                forward,
                [whole, whole] + partial,
                top,
                bottom,
                size,
                scal,
                *olds,
                high_turned,
                low_turned,
                step=step,
                flops=flops,
            )
            directions.append(d)
        gradients.append(g)
        hops = unit_terms(*terms)
        olds = [images[-1], scal] if step else []
        if step + 1 < ITERS:
            piece = shape(half * (rows + 2), LANES)
            image, scal, mine, theirs = call(
                back,
                [image_shape, vector, piece, piece],
                *hops,
                *olds,
                high,
                low,
                later=step > 0,
                flops=flops,
            )
            images.append(image)
            spread, size = sum_samples(mine + swap(theirs), scal)
            sizes.append(size)
        else:
            *parts, token = call(
                prepare,
                [shape(outputs, units)] * 3 + [image_shape, vector],
                core,
                *sizes,
                *directions,
                gradients[-1],
                *images,
                turned,
                specs=[smem] + [VMEM] * 8,
                scratch=[pltpu.VMEM((outputs * rows, LANES), F32)],
                flops=flops // 4,
            )
            image, scal, squares = call(
                last_image, [image_shape, vector, shape(chips, LANES)], *hops, *olds, token
            )
    all_chips = [[chip * CORES + c for chip in range(chips)] for c in range(CORES)]
    squares = lax.all_to_all(
        squares.reshape(chips, 1, LANES),
        "samp",
        0,
        0,
        axis_index_groups=all_chips,
        tiled=True,
    ).reshape(chips, LANES)
    readout, residual = call(
        finish,
        [shape(outputs, units), image_shape],
        core,
        squares,
        swap(squares),
        scal,
        image,
        *parts,
        specs=[smem] + [VMEM] * 8,
    )
    return readout.T, residual.T


def solution(mesh):
    return jax.shard_map(
        shards,
        mesh=mesh,
        in_specs=(P("samp", "unit"), P("samp", None)),
        out_specs=(P("unit", None), P("samp", None)),
        check_vma=False,
    )
```

```python
import functools

import jax
import jax.numpy as jnp
from jax import lax
from jax.experimental import pallas as pl
from jax.experimental.pallas import tpu as pltpu
from jax.sharding import PartitionSpec as P

ITERS = 3
ridge = 0.5
CORES, BLOCK, LANES, TILE = 2, 8, 128, 8
WIDE, FETCH = 256, 512
MIB = 1 << 20
F32, BF16 = jnp.float32, jnp.bfloat16
VMEM = pl.BlockSpec(memory_space=pltpu.VMEM)
HBM = pl.BlockSpec(memory_space=pl.ANY)


def shape(*dims, dtype=F32):
    return jax.ShapeDtypeStruct(dims, dtype)


def here(x):
    return pltpu.with_memory_space_constraint(x, pltpu.VMEM)


def call(kernel, out_shape, *args, scratch=(), limit=24, specs=None, flops=0, **static):
    return pl.pallas_call(
        functools.partial(kernel, **static),
        in_specs=specs or [VMEM] * len(args),
        out_specs=jax.tree.map(lambda _: VMEM, out_shape),
        out_shape=out_shape,
        scratch_shapes=list(scratch),
        compiler_params=pltpu.CompilerParams(vmem_limit_bytes=limit * MIB),
        cost_estimate=pl.CostEstimate(flops=flops, bytes_accessed=MIB, transcendentals=0),
        name=kernel.__name__,
    )(*args)


def split2(x):
    high = x.astype(BF16)
    return jnp.concatenate([high, (x - high.astype(F32)).astype(BF16)], axis=0)


def dot(a, b, ca, cb):
    return lax.dot_general(a, b, (((ca,), (cb,)), ((), ())), preferred_element_type=F32)


def fold(p):
    n = p.shape[0] // 2
    return p[n:] + p[:n]


def rows_product(x, high, low, at):
    x2 = split2(x) if x.dtype == F32 else x
    return fold(dot(x2, low[:, at], 1, 0) + dot(x2, high[:, at], 1, 0))


def row(x):
    return jnp.broadcast_to(x, (1, LANES))


def store_pieces(mine, theirs, value, at, stride):
    half = value.shape[0] // CORES
    for i in range(WIDE // LANES):
        part = value[:, i * LANES : (i + 1) * LANES]
        j = at * (WIDE // LANES) + i
        mine[pl.ds(j, half, stride=stride), :] = part[:half]
        theirs[pl.ds(j, half, stride=stride), :] = part[half:]


def own_half_first(x, own):
    half = x.shape[0] // CORES
    top, bottom = x[:half], x[half:]
    return jnp.concatenate(
        [jnp.where(own, top, bottom), jnp.where(own, bottom, top)], axis=0
    )


def first(core, states, targets, high, low, turned, mine, theirs, buf, target_buf, sems):
    steps = buf.shape[0]
    fetch = pltpu.make_async_copy(targets, target_buf, sems.at[steps])
    fetch.start()
    copies = [
        pltpu.make_async_copy(
            states.at[:, pl.ds(t * FETCH, FETCH)], buf.at[t], sems.at[t]
        )
        for t in range(steps)
    ]
    for c in copies:
        c.start()
    fetch.wait()
    x = own_half_first(target_buf[...], core[0, 0] == 0)
    turned[...] = x
    x2 = split2(x)
    half = x.shape[0] // CORES
    for t in range(steps):
        copies[t].wait()
        s = buf[t]
        h = s.astype(BF16)
        l = (s - h.astype(F32)).astype(BF16)
        high[:, pl.ds(t * FETCH, FETCH)] = h
        low[:, pl.ds(t * FETCH, FETCH)] = l
        p = fold(dot(x2, l, 1, 0) + dot(x2, h, 1, 0))
        for i in range(FETCH // WIDE):
            part = p[:, i * WIDE : (i + 1) * WIDE]
            store_pieces(mine, theirs, part, t * (FETCH // WIDE) + i, mine.shape[0] // half)


def turn_states(x, turned, token):
    turned[...] = x[...].T
    token[...] = jnp.zeros(token.shape, F32)


def combine(a, ra, b, rb):
    n = b.shape[0]
    image = jnp.concatenate([a[:n, :] + ra[:n, :], b[...] + rb[...]], axis=1)
    return image, a[n : n + TILE, :LANES] + ra[n : n + TILE, :LANES]


def step_image(hops, before, scal, image_out, scal_out):
    image, tail = combine(*hops)
    gamma = tail[0:1]
    if before is None:
        beta = jnp.zeros_like(gamma)
        square = gamma
    else:
        beta = gamma / scal[0:1, :]
        square = gamma + beta * (2.0 * tail[1:2] + beta * scal[2:3, :])
        image = image + beta[:, :1] * before[...]
    image_out[...] = image
    scal_out[0:1, :] = gamma
    scal_out[1:2, :] = beta
    scal_out[2:3, :] = square
    scal_out[3:, :] = jnp.zeros((TILE - 3, LANES), F32)
    return image, row(jnp.sum(image * image))


def back(*refs, later):
    hops = refs[:4]
    before, scal = refs[4:6] if later else (None, None)
    high, low, image_out, scal_out, mine, theirs = refs[-6:]
    image, image_sq = step_image(hops, before, scal, image_out, scal_out)
    half = image.shape[0] // CORES
    stride = mine.shape[0] // half
    x2 = split2(image)
    for t in range(high.shape[1] // WIDE):
        p = rows_product(x2, high, low, pl.ds(t * WIDE, WIDE))
        store_pieces(mine, theirs, p, t, stride)
    extra = jnp.broadcast_to(image_sq, (half, LANES))
    for j in range(high.shape[1] // LANES, stride):
        mine[pl.ds(j, half, stride=stride), :] = extra
        theirs[pl.ds(j, half, stride=stride), :] = extra


def last_image(h0, h1, h2, h3, before, scal, token, image_out, scal_out, squares):
    _, image_sq = step_image((h0, h1, h2, h3), before, scal, image_out, scal_out)
    squares[...] = jnp.broadcast_to(image_sq, squares.shape)


def step_size(image_sq, scal):
    return scal[0:1, :] / (image_sq + ridge * scal[2:3, :])


def add_pieces(a, b, token, out):
    out[...] = a[...] + b[...]


def sum_pieces(got, out):
    n = out.shape[0]
    terms = [got[i * n : (i + 1) * n, :] for i in range(got.shape[0] // n)]
    while len(terms) > 1:
        terms = [terms[i] + terms[i + 1] for i in range(0, len(terms), 2)]
    out[...] = terms[0]


def sum_blocks(*refs, rows, copies):
    t0, t1, t2, t3, *rest = refs
    total = (t0[...] + t2[...]) + (t1[...] + t3[...])
    out = rest[-2] if len(rest) == 3 else rest[-1]
    n = out.shape[0] // copies
    stride = total.shape[0] // (n // rows)
    for i in range(n // rows):
        part = total[i * stride : i * stride + rows]
        for k in range(copies):
            out[k * n + i * rows : k * n + (i + 1) * rows, :] = part
    if len(rest) == 3:
        scal, _, size = rest
        size[...] = jnp.broadcast_to(step_size(total[rows : rows + 1], scal), size.shape)


def forward(*refs, step):
    if step == 0:
        top, bottom, high, low, gradient, a, b = refs
        g = jnp.concatenate([top[...], bottom[...]], axis=0)
        cross = None
    else:
        if step == 1:
            top, bottom, size, scal, g_old, high, low, gradient, direction, a, b = refs
            d = g_old[...]
        else:
            top, bottom, size, scal, g_old, d_old, high, low, gradient, direction, a, b = refs
            d = g_old[...] + scal[1:2, :] * d_old[...]
        q = jnp.concatenate([top[...], bottom[...]], axis=0)
        direction[...] = d
        g = g_old[...] - size[0:1, :] * (q + ridge * d)
        cross = jnp.sum(g * d)
    gradient[...] = g
    n = b.shape[0]
    stride = g.shape[0] // n
    x2 = split2(
        jnp.concatenate([gradient[pl.ds(j, n, stride=stride), :] for j in range(stride)], axis=1)
    )
    steps = high.shape[1] // WIDE
    for t in range(steps):
        p = rows_product(x2, high, low, pl.ds(t * WIDE, WIDE))
        out, k = (a, t) if t < steps // 2 else (b, t - steps // 2)
        out[0:n, k * WIDE : (k + 1) * WIDE] = p
    a[n : n + 1, :] = jnp.broadcast_to(jnp.sum(g * g), (1, a.shape[1]))
    rest = jnp.zeros((TILE - 1, a.shape[1]), F32)
    a[n + 1 :, :] = rest if cross is None else rest + cross


def prepare(core, size0, size1, d0, d1, g2, i0, i1, targets, readout, before, gradient, residual, token, sums):
    own = core[0, 0] == 0
    n = targets.shape[0]
    stride = d0.shape[0] // n
    s0, s1 = size0[0:1, :], size1[0:1, :]
    sums[...] = s0 * d0[...] + s1 * d1[...]
    for source, out in ((sums, readout), (d1, before), (g2, gradient)):
        for j in range(stride):
            out[:, pl.ds(j * LANES, LANES)] = own_half_first(
                source[pl.ds(j, n, stride=stride), :], own
            )
    r = targets[...] - s0[:, :1] * i0[...] - s1[:, :1] * i1[...]
    residual[...] = own_half_first(r, own)
    token[...] = jnp.zeros(token.shape, F32)


def finish(core, squares, others, scal, image, readout_part, before, gradient, residual_part, readout, residual):
    image_sq = jnp.sum(squares[...] + others[...], axis=0, keepdims=True)
    size = step_size(image_sq, scal)[:, :1]
    beta = scal[1:2, :1]
    readout[...] = readout_part[...] + size * (gradient[...] + beta * before[...])
    last = own_half_first(image[...], core[0, 0] == 0)
    residual[...] = residual_part[...] - size * last


def shards(states, targets):
    samples, units = states.shape
    outputs = targets.shape[1]
    samp_count = lax.axis_size("samp")
    unit_count = lax.axis_size("unit")
    chips = samp_count // CORES
    half = outputs // CORES
    rows = units // LANES
    vector = shape(TILE, LANES)
    core = jnp.full((1, 1), lax.axis_index("samp") % CORES, jnp.int32)

    swap_cores = [(i, i ^ 1) for i in range(samp_count)]
    blocks = chips // BLOCK
    assert blocks == 4
    groups = [
        [(block * BLOCK + chip) * CORES + c for chip in range(BLOCK)]
        for block in range(blocks)
        for c in range(CORES)
    ]

    def swap(x):
        return lax.ppermute(x, "samp", swap_cores)

    def exchange(x):
        n = x.shape[0]
        x = x.reshape(BLOCK, n // BLOCK, LANES)
        x = lax.all_to_all(x, "samp", 0, 0, axis_index_groups=groups, tiled=True)
        return x.reshape(n, LANES)

    def block_terms(x):
        step = BLOCK * CORES
        return [x] + [
            lax.ppermute(
                x, "samp", [(i, (i + d * step) % samp_count) for i in range(samp_count)]
            )
            for d in range(1, blocks)
        ]

    def sum_samples(pieces, scal):
        n = pieces.shape[0] // BLOCK
        terms = block_terms(call(sum_pieces, shape(n, LANES), exchange(pieces)))
        outs = [shape(half * rows, LANES)] + ([] if scal is None else [vector])
        scals = [] if scal is None else [scal]
        outs = call(sum_blocks, outs, *terms, *scals, rows=rows, copies=BLOCK)
        return outs[0], outs[-1]

    def unit_hop(x, mask):
        return lax.ppermute(x, "unit", [(i, i ^ mask) for i in range(unit_count)])

    def unit_terms(a, b):
        a, b = a + unit_hop(a, 1), b + unit_hop(b, 3)
        return a, unit_hop(a, 3), b, unit_hop(b, 1)

    image_shape = shape(outputs, samples)
    whole = shape(outputs * rows, LANES)
    partial = [shape(outputs + TILE, samples // 2), shape(outputs, samples // 2)]
    flops = 2 * 4 * samples * units * outputs

    smem = pl.BlockSpec(memory_space=pltpu.SMEM)
    high, low, turned, mine, theirs = call(
        first,
        [shape(samples, units, dtype=BF16)] * 2 + [image_shape] + [shape(half * rows, LANES)] * 2,
        core,
        pltpu.with_memory_space_constraint(states, pltpu.HBM),
        pltpu.with_memory_space_constraint(targets.T, pltpu.HBM),
        specs=[smem, HBM, HBM],
        scratch=[
            pltpu.VMEM((units // FETCH, samples, FETCH), F32),
            pltpu.VMEM((outputs, samples), F32),
            pltpu.SemaphoreType.DMA((units // FETCH + 1,)),
        ],
        limit=32,
        flops=flops,
    )
    high, low = here(high), here(low)
    (high_turned, token), (low_turned, _) = [
        call(turn_states, [shape(units, samples, dtype=BF16), vector], x, flops=flops)
        for x in (high, low)
    ]
    high_turned, low_turned = here(high_turned), here(low_turned)
    pieces = call(add_pieces, shape(half * rows, LANES), mine, swap(theirs), token)
    spread, _ = sum_samples(pieces, None)

    gradients, directions, images, sizes = [], [], [], []
    scal = size = None
    for step in range(ITERS):
        top = exchange(spread)
        bottom = swap(top)
        if step == 0:
            g, *terms = call(
                forward,
                [whole] + partial,
                top,
                bottom,
                high_turned,
                low_turned,
                step=0,
                flops=flops,
            )
        else:
            olds = [gradients[-1]] + ([directions[-1]] if step > 1 else [])
            g, d, *terms = call(
                forward,
                [whole, whole] + partial,
                top,
                bottom,
                size,
                scal,
                *olds,
                high_turned,
                low_turned,
                step=step,
                flops=flops,
            )
            directions.append(d)
        gradients.append(g)
        hops = unit_terms(*terms)
        olds = [images[-1], scal] if step else []
        if step + 1 < ITERS:
            piece = shape(half * (rows + 2), LANES)
            image, scal, mine, theirs = call(
                back,
                [image_shape, vector, piece, piece],
                *hops,
                *olds,
                high,
                low,
                later=step > 0,
                flops=flops,
            )
            images.append(image)
            spread, size = sum_samples(mine + swap(theirs), scal)
            sizes.append(size)
        else:
            *parts, token = call(
                prepare,
                [shape(outputs, units)] * 3 + [image_shape, vector],
                core,
                *sizes,
                *directions,
                gradients[-1],
                *images,
                turned,
                specs=[smem] + [VMEM] * 8,
                scratch=[pltpu.VMEM((outputs * rows, LANES), F32)],
                flops=flops // 4,
            )
            image, scal, squares = call(
                last_image, [image_shape, vector, shape(chips, LANES)], *hops, *olds, token
            )
    all_chips = [[chip * CORES + c for chip in range(chips)] for c in range(CORES)]
    squares = lax.all_to_all(
        squares.reshape(chips, 1, LANES),
        "samp",
        0,
        0,
        axis_index_groups=all_chips,
        tiled=True,
    ).reshape(chips, LANES)
    readout, residual = call(
        finish,
        [shape(outputs, units), image_shape],
        core,
        squares,
        swap(squares),
        scal,
        image,
        *parts,
        specs=[smem] + [VMEM] * 8,
    )
    return readout.T, residual.T


def solution(mesh):
    return jax.shard_map(
        shards,
        mesh=mesh,
        in_specs=(P("samp", "unit"), P("samp", None)),
        out_specs=(P("unit", None), P("samp", None)),
        check_vma=False,
    )
```

```python
import functools

import jax
import jax.numpy as jnp
from jax import lax
from jax.experimental import pallas as pl
from jax.experimental.pallas import tpu as pltpu
from jax.sharding import PartitionSpec as P

ITERS = 3
ridge = 0.5
CORES, BLOCK, LANES, TILE = 2, 8, 128, 8
WIDE, FETCH = 256, 512
MIB = 1 << 20
F32, BF16 = jnp.float32, jnp.bfloat16
VMEM = pl.BlockSpec(memory_space=pltpu.VMEM)
HBM = pl.BlockSpec(memory_space=pl.ANY)


def shape(*dims, dtype=F32):
    return jax.ShapeDtypeStruct(dims, dtype)


def here(x):
    return pltpu.with_memory_space_constraint(x, pltpu.VMEM)


def call(kernel, out_shape, *args, scratch=(), limit=24, specs=None, flops=0, **static):
    return pl.pallas_call(
        functools.partial(kernel, **static),
        in_specs=specs or [VMEM] * len(args),
        out_specs=jax.tree.map(lambda _: VMEM, out_shape),
        out_shape=out_shape,
        scratch_shapes=list(scratch),
        compiler_params=pltpu.CompilerParams(vmem_limit_bytes=limit * MIB),
        cost_estimate=pl.CostEstimate(flops=flops, bytes_accessed=MIB, transcendentals=0),
        name=kernel.__name__,
    )(*args)


def split3(x):
    terms = []
    for _ in range(2):
        terms.append(x.astype(BF16))
        x = x - terms[-1].astype(F32)
    return jnp.concatenate(terms + [x.astype(BF16)], axis=0)


def dot(a, b, ca, cb):
    return lax.dot_general(a, b, (((ca,), (cb,)), ((), ())), preferred_element_type=F32)


def rows_product(x3, high, low):
    n = x3.shape[0] // 3
    p = dot(x3[: 2 * n], low, 1, 0)
    q = dot(x3, high, 1, 0)
    return q[:n] + ((p[:n] + q[n : 2 * n]) + (p[n:] + q[2 * n :]))


def row(x):
    return jnp.broadcast_to(x, (1, LANES))


def store_pieces(mine, theirs, value, at, stride):
    half = value.shape[0] // CORES
    for i in range(WIDE // LANES):
        part = value[:, i * LANES : (i + 1) * LANES]
        j = at * (WIDE // LANES) + i
        mine[pl.ds(j, half, stride=stride), :] = part[:half]
        theirs[pl.ds(j, half, stride=stride), :] = part[half:]


def own_half_first(x, own):
    half = x.shape[0] // CORES
    top, bottom = x[:half], x[half:]
    return jnp.concatenate(
        [jnp.where(own, top, bottom), jnp.where(own, bottom, top)], axis=0
    )


def first(core, states, targets, high, low, turned, mine, theirs, buf, target_buf, sems):
    steps = buf.shape[0]
    fetch = pltpu.make_async_copy(targets, target_buf, sems.at[steps])
    fetch.start()
    copies = [
        pltpu.make_async_copy(
            states.at[:, pl.ds(t * FETCH, FETCH)], buf.at[t], sems.at[t]
        )
        for t in range(steps)
    ]
    for c in copies:
        c.start()
    fetch.wait()
    x = own_half_first(target_buf[...], core[0, 0] == 0)
    turned[...] = x
    x3 = split3(x)
    half = x.shape[0] // CORES
    for t in range(steps):
        copies[t].wait()
        s = buf[t]
        h = s.astype(BF16)
        l = (s - h.astype(F32)).astype(BF16)
        high[:, pl.ds(t * FETCH, FETCH)] = h
        low[:, pl.ds(t * FETCH, FETCH)] = l
        p = rows_product(x3, h, l)
        for i in range(FETCH // WIDE):
            part = p[:, i * WIDE : (i + 1) * WIDE]
            store_pieces(mine, theirs, part, t * (FETCH // WIDE) + i, mine.shape[0] // half)


def turn_states(x, turned, token):
    turned[...] = x[...].T
    token[...] = jnp.zeros(token.shape, F32)


def combine(a, ra, b, rb):
    n = b.shape[0]
    image = jnp.concatenate([a[:n, :] + ra[:n, :], b[...] + rb[...]], axis=1)
    return image, a[n : n + TILE, :LANES] + ra[n : n + TILE, :LANES]


def step_image(hops, before, scal, image_out, scal_out):
    image, tail = combine(*hops)
    gamma = tail[0:1]
    if before is None:
        beta = jnp.zeros_like(gamma)
        square = gamma
    else:
        beta = gamma / scal[0:1, :]
        square = gamma + beta * (2.0 * tail[1:2] + beta * scal[2:3, :])
        image = image + beta[:, :1] * before[...]
    image_out[...] = image
    scal_out[0:1, :] = gamma
    scal_out[1:2, :] = beta
    scal_out[2:3, :] = square
    scal_out[3:, :] = jnp.zeros((TILE - 3, LANES), F32)
    return image, row(jnp.sum(image * image))


def back(*refs, later):
    hops = refs[:4]
    before, scal = refs[4:6] if later else (None, None)
    high, low, image_out, scal_out, mine, theirs = refs[-6:]
    image, image_sq = step_image(hops, before, scal, image_out, scal_out)
    half = image.shape[0] // CORES
    stride = mine.shape[0] // half
    x3 = split3(image)
    for t in range(high.shape[1] // WIDE):
        at = pl.ds(t * WIDE, WIDE)
        p = rows_product(x3, high[:, at], low[:, at])
        store_pieces(mine, theirs, p, t, stride)
    extra = jnp.broadcast_to(image_sq, (half, LANES))
    for j in range(high.shape[1] // LANES, stride):
        mine[pl.ds(j, half, stride=stride), :] = extra
        theirs[pl.ds(j, half, stride=stride), :] = extra


def last_image(h0, h1, h2, h3, before, scal, token, image_out, scal_out, squares):
    _, image_sq = step_image((h0, h1, h2, h3), before, scal, image_out, scal_out)
    squares[...] = jnp.broadcast_to(image_sq, squares.shape)


def step_size(image_sq, scal):
    return scal[0:1, :] / (image_sq + ridge * scal[2:3, :])


def add_pieces(a, b, token, out):
    out[...] = a[...] + b[...]


def sum_pieces(got, out):
    n = out.shape[0]
    terms = [got[i * n : (i + 1) * n, :] for i in range(got.shape[0] // n)]
    while len(terms) > 1:
        terms = [terms[i] + terms[i + 1] for i in range(0, len(terms), 2)]
    out[...] = terms[0]


def sum_blocks(*refs, rows, copies):
    t0, t1, t2, t3, *rest = refs
    total = (t0[...] + t2[...]) + (t1[...] + t3[...])
    out = rest[-2] if len(rest) == 3 else rest[-1]
    n = out.shape[0] // copies
    stride = total.shape[0] // (n // rows)
    for i in range(n // rows):
        part = total[i * stride : i * stride + rows]
        for k in range(copies):
            out[k * n + i * rows : k * n + (i + 1) * rows, :] = part
    if len(rest) == 3:
        scal, _, size = rest
        size[...] = jnp.broadcast_to(step_size(total[rows : rows + 1], scal), size.shape)


def forward(*refs, step):
    if step == 0:
        top, bottom, high, low, gradient, a, b = refs
        g = jnp.concatenate([top[...], bottom[...]], axis=0)
        cross = None
    else:
        if step == 1:
            top, bottom, size, scal, g_old, high, low, gradient, direction, a, b = refs
            d = g_old[...]
        else:
            top, bottom, size, scal, g_old, d_old, high, low, gradient, direction, a, b = refs
            d = g_old[...] + scal[1:2, :] * d_old[...]
        q = jnp.concatenate([top[...], bottom[...]], axis=0)
        direction[...] = d
        g = g_old[...] - size[0:1, :] * (q + ridge * d)
        cross = jnp.sum(g * d)
    gradient[...] = g
    n = b.shape[0]
    stride = g.shape[0] // n
    x3 = split3(
        jnp.concatenate([gradient[pl.ds(j, n, stride=stride), :] for j in range(stride)], axis=1)
    )
    steps = high.shape[1] // WIDE
    for t in range(steps):
        at = pl.ds(t * WIDE, WIDE)
        p = rows_product(x3, high[:, at], low[:, at])
        out, k = (a, t) if t < steps // 2 else (b, t - steps // 2)
        out[0:n, k * WIDE : (k + 1) * WIDE] = p
    a[n : n + 1, :] = jnp.broadcast_to(jnp.sum(g * g), (1, a.shape[1]))
    rest = jnp.zeros((TILE - 1, a.shape[1]), F32)
    a[n + 1 :, :] = rest if cross is None else rest + cross


def prepare(core, size0, size1, d0, d1, g2, i0, i1, targets, readout, before, gradient, residual, token, sums):
    own = core[0, 0] == 0
    n = targets.shape[0]
    stride = d0.shape[0] // n
    s0, s1 = size0[0:1, :], size1[0:1, :]
    sums[...] = s0 * d0[...] + s1 * d1[...]
    for source, out in ((sums, readout), (d1, before), (g2, gradient)):
        for j in range(stride):
            out[:, pl.ds(j * LANES, LANES)] = own_half_first(
                source[pl.ds(j, n, stride=stride), :], own
            )
    r = targets[...] - s0[:, :1] * i0[...] - s1[:, :1] * i1[...]
    residual[...] = own_half_first(r, own)
    token[...] = jnp.zeros(token.shape, F32)


def finish(core, squares, others, scal, image, readout_part, before, gradient, residual_part, readout, residual):
    image_sq = jnp.sum(squares[...] + others[...], axis=0, keepdims=True)
    size = step_size(image_sq, scal)[:, :1]
    beta = scal[1:2, :1]
    readout[...] = readout_part[...] + size * (gradient[...] + beta * before[...])
    last = own_half_first(image[...], core[0, 0] == 0)
    residual[...] = residual_part[...] - size * last


def shards(states, targets):
    samples, units = states.shape
    outputs = targets.shape[1]
    samp_count = lax.axis_size("samp")
    unit_count = lax.axis_size("unit")
    chips = samp_count // CORES
    half = outputs // CORES
    rows = units // LANES
    vector = shape(TILE, LANES)
    core = jnp.full((1, 1), lax.axis_index("samp") % CORES, jnp.int32)

    swap_cores = [(i, i ^ 1) for i in range(samp_count)]
    blocks = chips // BLOCK
    assert blocks == 4
    groups = [
        [(block * BLOCK + chip) * CORES + c for chip in range(BLOCK)]
        for block in range(blocks)
        for c in range(CORES)
    ]

    def swap(x):
        return lax.ppermute(x, "samp", swap_cores)

    def exchange(x):
        n = x.shape[0]
        x = x.reshape(BLOCK, n // BLOCK, LANES)
        x = lax.all_to_all(x, "samp", 0, 0, axis_index_groups=groups, tiled=True)
        return x.reshape(n, LANES)

    def block_terms(x):
        step = BLOCK * CORES
        return [x] + [
            lax.ppermute(
                x, "samp", [(i, (i + d * step) % samp_count) for i in range(samp_count)]
            )
            for d in range(1, blocks)
        ]

    def sum_samples(pieces, scal):
        n = pieces.shape[0] // BLOCK
        terms = block_terms(call(sum_pieces, shape(n, LANES), exchange(pieces)))
        outs = [shape(half * rows, LANES)] + ([] if scal is None else [vector])
        scals = [] if scal is None else [scal]
        outs = call(sum_blocks, outs, *terms, *scals, rows=rows, copies=BLOCK)
        return outs[0], outs[-1]

    def unit_hop(x, mask):
        return lax.ppermute(x, "unit", [(i, i ^ mask) for i in range(unit_count)])

    def unit_terms(a, b):
        a, b = a + unit_hop(a, 1), b + unit_hop(b, 3)
        return a, unit_hop(a, 3), b, unit_hop(b, 1)

    image_shape = shape(outputs, samples)
    whole = shape(outputs * rows, LANES)
    partial = [shape(outputs + TILE, samples // 2), shape(outputs, samples // 2)]
    flops = 2 * 4 * samples * units * outputs

    smem = pl.BlockSpec(memory_space=pltpu.SMEM)
    high, low, turned, mine, theirs = call(
        first,
        [shape(samples, units, dtype=BF16)] * 2 + [image_shape] + [shape(half * rows, LANES)] * 2,
        core,
        pltpu.with_memory_space_constraint(states, pltpu.HBM),
        pltpu.with_memory_space_constraint(targets.T, pltpu.HBM),
        specs=[smem, HBM, HBM],
        scratch=[
            pltpu.VMEM((units // FETCH, samples, FETCH), F32),
            pltpu.VMEM((outputs, samples), F32),
            pltpu.SemaphoreType.DMA((units // FETCH + 1,)),
        ],
        limit=32,
        flops=flops,
    )
    high, low = here(high), here(low)
    (high_turned, token), (low_turned, _) = [
        call(turn_states, [shape(units, samples, dtype=BF16), vector], x, flops=flops)
        for x in (high, low)
    ]
    high_turned, low_turned = here(high_turned), here(low_turned)
    pieces = call(add_pieces, shape(half * rows, LANES), mine, swap(theirs), token)
    spread, _ = sum_samples(pieces, None)

    gradients, directions, images, sizes = [], [], [], []
    scal = size = None
    for step in range(ITERS):
        top = exchange(spread)
        bottom = swap(top)
        if step == 0:
            g, *terms = call(
                forward,
                [whole] + partial,
                top,
                bottom,
                high_turned,
                low_turned,
                step=0,
                flops=flops,
            )
        else:
            olds = [gradients[-1]] + ([directions[-1]] if step > 1 else [])
            g, d, *terms = call(
                forward,
                [whole, whole] + partial,
                top,
                bottom,
                size,
                scal,
                *olds,
                high_turned,
                low_turned,
                step=step,
                flops=flops,
            )
            directions.append(d)
        gradients.append(g)
        hops = unit_terms(*terms)
        olds = [images[-1], scal] if step else []
        if step + 1 < ITERS:
            piece = shape(half * (rows + 2), LANES)
            image, scal, mine, theirs = call(
                back,
                [image_shape, vector, piece, piece],
                *hops,
                *olds,
                high,
                low,
                later=step > 0,
                flops=flops,
            )
            images.append(image)
            spread, size = sum_samples(mine + swap(theirs), scal)
            sizes.append(size)
        else:
            *parts, token = call(
                prepare,
                [shape(outputs, units)] * 3 + [image_shape, vector],
                core,
                *sizes,
                *directions,
                gradients[-1],
                *images,
                turned,
                specs=[smem] + [VMEM] * 8,
                scratch=[pltpu.VMEM((outputs * rows, LANES), F32)],
                flops=flops // 4,
            )
            image, scal, squares = call(
                last_image, [image_shape, vector, shape(chips, LANES)], *hops, *olds, token
            )
    all_chips = [[chip * CORES + c for chip in range(chips)] for c in range(CORES)]
    squares = lax.all_to_all(
        squares.reshape(chips, 1, LANES),
        "samp",
        0,
        0,
        axis_index_groups=all_chips,
        tiled=True,
    ).reshape(chips, LANES)
    readout, residual = call(
        finish,
        [shape(outputs, units), image_shape],
        core,
        squares,
        swap(squares),
        scal,
        image,
        *parts,
        specs=[smem] + [VMEM] * 8,
    )
    return readout.T, residual.T


def solution(mesh):
    return jax.shard_map(
        shards,
        mesh=mesh,
        in_specs=(P("samp", "unit"), P("samp", None)),
        out_specs=(P("unit", None), P("samp", None)),
        check_vma=False,
    )
```

```python
import functools

import jax
import jax.numpy as jnp
from jax import lax
from jax.experimental import pallas as pl
from jax.experimental.pallas import tpu as pltpu
from jax.sharding import PartitionSpec as P

ITERS = 3
ridge = 0.5
CORES, BLOCK, LANES, TILE = 2, 8, 128, 8
WIDE, FETCH = 256, 512
MIB = 1 << 20
F32, BF16 = jnp.float32, jnp.bfloat16
VMEM = pl.BlockSpec(memory_space=pltpu.VMEM)
HBM = pl.BlockSpec(memory_space=pl.ANY)


def shape(*dims, dtype=F32):
    return jax.ShapeDtypeStruct(dims, dtype)


def here(x):
    return pltpu.with_memory_space_constraint(x, pltpu.VMEM)


def call(kernel, out_shape, *args, scratch=(), limit=24, specs=None, flops=0, **static):
    return pl.pallas_call(
        functools.partial(kernel, **static),
        in_specs=specs or [VMEM] * len(args),
        out_specs=jax.tree.map(lambda _: VMEM, out_shape),
        out_shape=out_shape,
        scratch_shapes=list(scratch),
        compiler_params=pltpu.CompilerParams(vmem_limit_bytes=limit * MIB),
        cost_estimate=pl.CostEstimate(flops=flops, bytes_accessed=MIB, transcendentals=0),
        name=kernel.__name__,
    )(*args)


def split3(x):
    terms = []
    for _ in range(2):
        terms.append(x.astype(BF16))
        x = x - terms[-1].astype(F32)
    return jnp.concatenate(terms + [x.astype(BF16)], axis=0)


def dot(a, b, ca, cb):
    return lax.dot_general(a, b, (((ca,), (cb,)), ((), ())), preferred_element_type=F32)


def rows_product(x3, high, low):
    n = x3.shape[0] // 3
    p = dot(x3[: 2 * n], low, 1, 0)
    q = dot(x3, high, 1, 0)
    return q[:n] + ((p[:n] + q[n : 2 * n]) + (p[n:] + q[2 * n :]))


def row(x):
    return jnp.broadcast_to(x, (1, LANES))


def store_pieces(mine, theirs, value, at, stride):
    half = value.shape[0] // CORES
    for i in range(WIDE // LANES):
        part = value[:, i * LANES : (i + 1) * LANES]
        j = at * (WIDE // LANES) + i
        mine[pl.ds(j, half, stride=stride), :] = part[:half]
        theirs[pl.ds(j, half, stride=stride), :] = part[half:]


def own_half_first(x, own):
    half = x.shape[0] // CORES
    top, bottom = x[:half], x[half:]
    return jnp.concatenate(
        [jnp.where(own, top, bottom), jnp.where(own, bottom, top)], axis=0
    )


def first(core, states, targets, high, low, turned, mine, theirs, buf, target_buf, sems):
    steps = buf.shape[0]
    fetch = pltpu.make_async_copy(targets, target_buf, sems.at[steps])
    fetch.start()
    copies = [
        pltpu.make_async_copy(
            states.at[:, pl.ds(t * FETCH, FETCH)], buf.at[t], sems.at[t]
        )
        for t in range(steps)
    ]
    for c in copies:
        c.start()
    fetch.wait()
    x = own_half_first(target_buf[...], core[0, 0] == 0)
    turned[...] = x
    x3 = split3(x)
    half = x.shape[0] // CORES
    for t in range(steps):
        copies[t].wait()
        s = buf[t]
        h = s.astype(BF16)
        l = (s - h.astype(F32)).astype(BF16)
        high[:, pl.ds(t * FETCH, FETCH)] = h
        low[:, pl.ds(t * FETCH, FETCH)] = l
        p = rows_product(x3, h, l)
        for i in range(FETCH // WIDE):
            part = p[:, i * WIDE : (i + 1) * WIDE]
            store_pieces(mine, theirs, part, t * (FETCH // WIDE) + i, mine.shape[0] // half)


def turn_states(x, turned, token):
    turned[...] = x[...].T
    token[...] = jnp.zeros(token.shape, F32)


def combine(a, ra, b, rb, n):
    tiles = b.shape[0] // n
    parts = []
    for x, rx in ((a, ra), (b, rb)):
        parts += [x[j * n : (j + 1) * n, :] + rx[j * n : (j + 1) * n, :] for j in range(tiles)]
    image = jnp.concatenate(parts, axis=1)
    return image, a[tiles * n :, :] + ra[tiles * n :, :]


def step_image(hops, before, scal, image_out, scal_out):
    image, tail = combine(*hops, image_out.shape[0])
    gamma = tail[0:1]
    if before is None:
        beta = jnp.zeros_like(gamma)
        square = gamma
    else:
        beta = gamma / scal[0:1, :]
        square = gamma + beta * (2.0 * tail[1:2] + beta * scal[2:3, :])
        image = image + beta[:, :1] * before[...]
    image_out[...] = image
    scal_out[0:1, :] = gamma
    scal_out[1:2, :] = beta
    scal_out[2:3, :] = square
    scal_out[3:, :] = jnp.zeros((TILE - 3, LANES), F32)
    return image, row(jnp.sum(image * image))


def back(*refs, later):
    hops = refs[:4]
    before, scal = refs[4:6] if later else (None, None)
    high, low, image_out, scal_out, mine, theirs = refs[-6:]
    image, image_sq = step_image(hops, before, scal, image_out, scal_out)
    half = image.shape[0] // CORES
    stride = mine.shape[0] // half
    x3 = split3(image)
    for t in range(high.shape[1] // WIDE):
        at = pl.ds(t * WIDE, WIDE)
        p = rows_product(x3, high[:, at], low[:, at])
        store_pieces(mine, theirs, p, t, stride)
    extra = jnp.broadcast_to(image_sq, (half, LANES))
    for j in range(high.shape[1] // LANES, stride):
        mine[pl.ds(j, half, stride=stride), :] = extra
        theirs[pl.ds(j, half, stride=stride), :] = extra


def last_image(h0, h1, h2, h3, before, scal, token, image_out, scal_out, squares):
    _, image_sq = step_image((h0, h1, h2, h3), before, scal, image_out, scal_out)
    squares[...] = jnp.broadcast_to(image_sq, squares.shape)


def step_size(image_sq, scal):
    return scal[0:1, :] / (image_sq + ridge * scal[2:3, :])


def add_pieces(a, b, token, out):
    out[...] = a[...] + b[...]


def sum_pieces(got, out):
    n = out.shape[0]
    terms = [got[i * n : (i + 1) * n, :] for i in range(got.shape[0] // n)]
    while len(terms) > 1:
        terms = [terms[i] + terms[i + 1] for i in range(0, len(terms), 2)]
    out[...] = terms[0]


def sum_blocks(*refs, rows, copies):
    t0, t1, t2, t3, *rest = refs
    total = (t0[...] + t2[...]) + (t1[...] + t3[...])
    out = rest[-2] if len(rest) == 3 else rest[-1]
    n = out.shape[0] // copies
    stride = total.shape[0] // (n // rows)
    for i in range(n // rows):
        part = total[i * stride : i * stride + rows]
        for k in range(copies):
            out[k * n + i * rows : k * n + (i + 1) * rows, :] = part
    if len(rest) == 3:
        scal, _, size = rest
        size[...] = jnp.broadcast_to(step_size(total[rows : rows + 1], scal), size.shape)


def forward(*refs, step):
    if step == 0:
        top, bottom, high, low, gradient, a, b = refs
        g = jnp.concatenate([top[...], bottom[...]], axis=0)
        cross = None
    else:
        if step == 1:
            top, bottom, size, scal, g_old, high, low, gradient, direction, a, b = refs
            d = g_old[...]
        else:
            top, bottom, size, scal, g_old, d_old, high, low, gradient, direction, a, b = refs
            d = g_old[...] + scal[1:2, :] * d_old[...]
        q = jnp.concatenate([top[...], bottom[...]], axis=0)
        direction[...] = d
        g = g_old[...] - size[0:1, :] * (q + ridge * d)
        cross = jnp.sum(g * d)
    gradient[...] = g
    stride = high.shape[0] // LANES
    n = g.shape[0] // stride
    x3 = split3(
        jnp.concatenate([gradient[pl.ds(j, n, stride=stride), :] for j in range(stride)], axis=1)
    )
    tiles = b.shape[0] // n
    for t in range(high.shape[1] // WIDE):
        at = pl.ds(t * WIDE, WIDE)
        p = rows_product(x3, high[:, at], low[:, at])
        for i in range(WIDE // LANES):
            j = t * (WIDE // LANES) + i
            out = a if j < tiles else b
            k = j % tiles
            out[k * n : (k + 1) * n, :] = p[:, i * LANES : (i + 1) * LANES]
    k = tiles * n
    a[k : k + 1, :] = row(jnp.sum(g * g))
    rest = jnp.zeros((TILE - 1, LANES), F32)
    a[k + 1 :, :] = rest if cross is None else rest + cross


def prepare(core, size0, size1, d0, d1, g2, i0, i1, targets, readout, before, gradient, residual, token, sums):
    own = core[0, 0] == 0
    n = targets.shape[0]
    stride = d0.shape[0] // n
    s0, s1 = size0[0:1, :], size1[0:1, :]
    sums[...] = s0 * d0[...] + s1 * d1[...]
    for source, out in ((sums, readout), (d1, before), (g2, gradient)):
        for j in range(stride):
            out[:, pl.ds(j * LANES, LANES)] = own_half_first(
                source[pl.ds(j, n, stride=stride), :], own
            )
    r = targets[...] - s0[:, :1] * i0[...] - s1[:, :1] * i1[...]
    residual[...] = own_half_first(r, own)
    token[...] = jnp.zeros(token.shape, F32)


def finish(core, squares, others, scal, image, readout_part, before, gradient, residual_part, readout, residual):
    image_sq = jnp.sum(squares[...] + others[...], axis=0, keepdims=True)
    size = step_size(image_sq, scal)[:, :1]
    beta = scal[1:2, :1]
    readout[...] = readout_part[...] + size * (gradient[...] + beta * before[...])
    last = own_half_first(image[...], core[0, 0] == 0)
    residual[...] = residual_part[...] - size * last


def shards(states, targets):
    samples, units = states.shape
    outputs = targets.shape[1]
    samp_count = lax.axis_size("samp")
    unit_count = lax.axis_size("unit")
    chips = samp_count // CORES
    half = outputs // CORES
    rows = units // LANES
    vector = shape(TILE, LANES)
    core = jnp.full((1, 1), lax.axis_index("samp") % CORES, jnp.int32)

    swap_cores = [(i, i ^ 1) for i in range(samp_count)]
    blocks = chips // BLOCK
    assert blocks == 4
    groups = [
        [(block * BLOCK + chip) * CORES + c for chip in range(BLOCK)]
        for block in range(blocks)
        for c in range(CORES)
    ]

    def swap(x):
        return lax.ppermute(x, "samp", swap_cores)

    def exchange(x):
        n = x.shape[0]
        x = x.reshape(BLOCK, n // BLOCK, LANES)
        x = lax.all_to_all(x, "samp", 0, 0, axis_index_groups=groups, tiled=True)
        return x.reshape(n, LANES)

    def block_terms(x):
        step = BLOCK * CORES
        return [x] + [
            lax.ppermute(
                x, "samp", [(i, (i + d * step) % samp_count) for i in range(samp_count)]
            )
            for d in range(1, blocks)
        ]

    def sum_samples(pieces, scal):
        n = pieces.shape[0] // BLOCK
        terms = block_terms(call(sum_pieces, shape(n, LANES), exchange(pieces)))
        outs = [shape(half * rows, LANES)] + ([] if scal is None else [vector])
        scals = [] if scal is None else [scal]
        outs = call(sum_blocks, outs, *terms, *scals, rows=rows, copies=BLOCK)
        return outs[0], outs[-1]

    def unit_hop(x, mask):
        return lax.ppermute(x, "unit", [(i, i ^ mask) for i in range(unit_count)])

    def unit_terms(a, b):
        a, b = a + unit_hop(a, 1), b + unit_hop(b, 3)
        return a, unit_hop(a, 3), b, unit_hop(b, 1)

    image_shape = shape(outputs, samples)
    whole = shape(outputs * rows, LANES)
    tiles = outputs * samples // 2 // LANES
    partial = [shape(tiles + TILE, LANES), shape(tiles, LANES)]
    flops = 2 * 4 * samples * units * outputs

    smem = pl.BlockSpec(memory_space=pltpu.SMEM)
    high, low, turned, mine, theirs = call(
        first,
        [shape(samples, units, dtype=BF16)] * 2 + [image_shape] + [shape(half * rows, LANES)] * 2,
        core,
        pltpu.with_memory_space_constraint(states, pltpu.HBM),
        pltpu.with_memory_space_constraint(targets.T, pltpu.HBM),
        specs=[smem, HBM, HBM],
        scratch=[
            pltpu.VMEM((units // FETCH, samples, FETCH), F32),
            pltpu.VMEM((outputs, samples), F32),
            pltpu.SemaphoreType.DMA((units // FETCH + 1,)),
        ],
        limit=32,
        flops=flops,
    )
    high, low = here(high), here(low)
    (high_turned, token), (low_turned, _) = [
        call(turn_states, [shape(units, samples, dtype=BF16), vector], x, flops=flops)
        for x in (high, low)
    ]
    high_turned, low_turned = here(high_turned), here(low_turned)
    pieces = call(add_pieces, shape(half * rows, LANES), mine, swap(theirs), token)
    spread, _ = sum_samples(pieces, None)

    gradients, directions, images, sizes = [], [], [], []
    scal = size = None
    for step in range(ITERS):
        top = exchange(spread)
        bottom = swap(top)
        if step == 0:
            g, *terms = call(
                forward,
                [whole] + partial,
                top,
                bottom,
                high_turned,
                low_turned,
                step=0,
                flops=flops,
            )
        else:
            olds = [gradients[-1]] + ([directions[-1]] if step > 1 else [])
            g, d, *terms = call(
                forward,
                [whole, whole] + partial,
                top,
                bottom,
                size,
                scal,
                *olds,
                high_turned,
                low_turned,
                step=step,
                flops=flops,
            )
            directions.append(d)
        gradients.append(g)
        hops = unit_terms(*terms)
        olds = [images[-1], scal] if step else []
        if step + 1 < ITERS:
            piece = shape(half * (rows + 2), LANES)
            image, scal, mine, theirs = call(
                back,
                [image_shape, vector, piece, piece],
                *hops,
                *olds,
                high,
                low,
                later=step > 0,
                flops=flops,
            )
            images.append(image)
            spread, size = sum_samples(mine + swap(theirs), scal)
            sizes.append(size)
        else:
            *parts, token = call(
                prepare,
                [shape(outputs, units)] * 3 + [image_shape, vector],
                core,
                *sizes,
                *directions,
                gradients[-1],
                *images,
                turned,
                specs=[smem] + [VMEM] * 8,
                scratch=[pltpu.VMEM((outputs * rows, LANES), F32)],
                flops=flops // 4,
            )
            image, scal, squares = call(
                last_image, [image_shape, vector, shape(chips, LANES)], *hops, *olds, token
            )
    all_chips = [[chip * CORES + c for chip in range(chips)] for c in range(CORES)]
    squares = lax.all_to_all(
        squares.reshape(chips, 1, LANES),
        "samp",
        0,
        0,
        axis_index_groups=all_chips,
        tiled=True,
    ).reshape(chips, LANES)
    readout, residual = call(
        finish,
        [shape(outputs, units), image_shape],
        core,
        squares,
        swap(squares),
        scal,
        image,
        *parts,
        specs=[smem] + [VMEM] * 8,
    )
    return readout.T, residual.T


def solution(mesh):
    return jax.shard_map(
        shards,
        mesh=mesh,
        in_specs=(P("samp", "unit"), P("samp", None)),
        out_specs=(P("unit", None), P("samp", None)),
        check_vma=False,
    )
```

```python
import functools

import jax
import jax.numpy as jnp
from jax import lax
from jax.experimental import pallas as pl
from jax.experimental.pallas import tpu as pltpu
from jax.sharding import PartitionSpec as P

ITERS = 3
ridge = 0.5
CORES, BLOCK, LANES, TILE = 2, 8, 128, 8
WIDE, FETCH = 256, 512
MIB = 1 << 20
F32, BF16 = jnp.float32, jnp.bfloat16
VMEM = pl.BlockSpec(memory_space=pltpu.VMEM)
HBM = pl.BlockSpec(memory_space=pl.ANY)


def shape(*dims, dtype=F32):
    return jax.ShapeDtypeStruct(dims, dtype)


def here(x):
    return pltpu.with_memory_space_constraint(x, pltpu.VMEM)


def call(kernel, out_shape, *args, scratch=(), limit=24, specs=None, outs=None, flops=0, **static):
    return pl.pallas_call(
        functools.partial(kernel, **static),
        in_specs=specs or [VMEM] * len(args),
        out_specs=outs or jax.tree.map(lambda _: VMEM, out_shape),
        out_shape=out_shape,
        scratch_shapes=list(scratch),
        compiler_params=pltpu.CompilerParams(vmem_limit_bytes=limit * MIB),
        cost_estimate=pl.CostEstimate(flops=flops, bytes_accessed=MIB, transcendentals=0),
        name=kernel.__name__,
    )(*args)


def split3(x):
    terms = []
    for _ in range(2):
        terms.append(x.astype(BF16))
        x = x - terms[-1].astype(F32)
    return jnp.concatenate(terms + [x.astype(BF16)], axis=0)


def dot(a, b, ca, cb):
    return lax.dot_general(a, b, (((ca,), (cb,)), ((), ())), preferred_element_type=F32)


def rows_product(x3, high, low):
    n = x3.shape[0] // 3
    p = dot(x3[: 2 * n], low, 1, 0)
    q = dot(x3, high, 1, 0)
    return q[:n] + ((p[:n] + q[n : 2 * n]) + (p[n:] + q[2 * n :]))


def row(x):
    return jnp.broadcast_to(x, (1, LANES))


def store_pieces(mine, theirs, value, at, stride):
    half = value.shape[0] // CORES
    for i in range(WIDE // LANES):
        part = value[:, i * LANES : (i + 1) * LANES]
        j = at * (WIDE // LANES) + i
        mine[pl.ds(j, half, stride=stride), :] = part[:half]
        theirs[pl.ds(j, half, stride=stride), :] = part[half:]


def own_half_first(x, own):
    half = x.shape[0] // CORES
    top, bottom = x[:half], x[half:]
    return jnp.concatenate(
        [jnp.where(own, top, bottom), jnp.where(own, bottom, top)], axis=0
    )


def first(core, states, targets, high, low, turned, mine, theirs, buf, target_buf, sems):
    steps = buf.shape[0]
    fetch = pltpu.make_async_copy(targets, target_buf, sems.at[steps])
    fetch.start()
    copies = [
        pltpu.make_async_copy(
            states.at[:, pl.ds(t * FETCH, FETCH)], buf.at[t], sems.at[t]
        )
        for t in range(steps)
    ]
    for c in copies:
        c.start()
    fetch.wait()
    x = own_half_first(target_buf[...], core[0, 0] == 0)
    turned[...] = x
    x3 = split3(x)
    half = x.shape[0] // CORES
    for t in range(steps):
        copies[t].wait()
        s = buf[t]
        h = s.astype(BF16)
        l = (s - h.astype(F32)).astype(BF16)
        high[:, pl.ds(t * FETCH, FETCH)] = h
        low[:, pl.ds(t * FETCH, FETCH)] = l
        p = rows_product(x3, h, l)
        for i in range(FETCH // WIDE):
            part = p[:, i * WIDE : (i + 1) * WIDE]
            store_pieces(mine, theirs, part, t * (FETCH // WIDE) + i, mine.shape[0] // half)


def turn_states(x, turned, token):
    turned[...] = x[...].T
    token[...] = jnp.zeros(token.shape, F32)


def combine(a, ra, b, rb, n):
    tiles = b.shape[0] // n
    parts = []
    for x, rx in ((a, ra), (b, rb)):
        parts += [x[j * n : (j + 1) * n, :] + rx[j * n : (j + 1) * n, :] for j in range(tiles)]
    image = jnp.concatenate(parts, axis=1)
    return image, a[tiles * n :, :] + ra[tiles * n :, :]


def step_image(hops, before, scal, image_out, scal_out):
    image, tail = combine(*hops, image_out.shape[0])
    gamma = tail[0:1]
    if before is None:
        beta = jnp.zeros_like(gamma)
        square = gamma
    else:
        beta = gamma / scal[0:1, :]
        square = gamma + beta * (2.0 * tail[1:2] + beta * scal[2:3, :])
        image = image + beta[:, :1] * before[...]
    image_out[...] = image
    scal_out[0:1, :] = gamma
    scal_out[1:2, :] = beta
    scal_out[2:3, :] = square
    scal_out[3:, :] = jnp.zeros((TILE - 3, LANES), F32)
    return image, row(jnp.sum(image * image))


def back(*refs, later):
    hops = refs[:4]
    before, scal = refs[4:6] if later else (None, None)
    high, low, image_out, scal_out, mine, theirs = refs[-6:]
    image, image_sq = step_image(hops, before, scal, image_out, scal_out)
    half = image.shape[0] // CORES
    stride = mine.shape[0] // half
    x3 = split3(image)
    for t in range(high.shape[1] // WIDE):
        at = pl.ds(t * WIDE, WIDE)
        p = rows_product(x3, high[:, at], low[:, at])
        store_pieces(mine, theirs, p, t, stride)
    extra = jnp.broadcast_to(image_sq, (half, LANES))
    for j in range(high.shape[1] // LANES, stride):
        mine[pl.ds(j, half, stride=stride), :] = extra
        theirs[pl.ds(j, half, stride=stride), :] = extra


def last_image(h0, h1, h2, h3, before, scal, token, image_out, scal_out, squares):
    _, image_sq = step_image((h0, h1, h2, h3), before, scal, image_out, scal_out)
    squares[...] = jnp.broadcast_to(image_sq, squares.shape)


def step_size(image_sq, scal):
    return scal[0:1, :] / (image_sq + ridge * scal[2:3, :])


def add_pieces(a, b, token, out):
    out[...] = a[...] + b[...]


def sum_pieces(got, out):
    n = out.shape[0]
    terms = [got[i * n : (i + 1) * n, :] for i in range(got.shape[0] // n)]
    while len(terms) > 1:
        terms = [terms[i] + terms[i + 1] for i in range(0, len(terms), 2)]
    out[...] = terms[0]


def sum_blocks(*refs, rows, copies):
    t0, t1, t2, t3, *rest = refs
    total = (t0[...] + t2[...]) + (t1[...] + t3[...])
    out = rest[-2] if len(rest) == 3 else rest[-1]
    n = out.shape[0] // copies
    stride = total.shape[0] // (n // rows)
    for i in range(n // rows):
        part = total[i * stride : i * stride + rows]
        for k in range(copies):
            out[k * n + i * rows : k * n + (i + 1) * rows, :] = part
    if len(rest) == 3:
        scal, _, size = rest
        size[...] = jnp.broadcast_to(step_size(total[rows : rows + 1], scal), size.shape)


def forward(*refs, step):
    if step == 0:
        top, bottom, high, low, gradient, a, b = refs
        g = jnp.concatenate([top[...], bottom[...]], axis=0)
        cross = None
    else:
        if step == 1:
            top, bottom, size, scal, g_old, high, low, gradient, direction, a, b = refs
            d = g_old[...]
        else:
            top, bottom, size, scal, g_old, d_old, high, low, gradient, direction, a, b = refs
            d = g_old[...] + scal[1:2, :] * d_old[...]
        q = jnp.concatenate([top[...], bottom[...]], axis=0)
        direction[...] = d
        g = g_old[...] - size[0:1, :] * (q + ridge * d)
        cross = jnp.sum(g * d)
    gradient[...] = g
    stride = high.shape[0] // LANES
    n = g.shape[0] // stride
    x3 = split3(
        jnp.concatenate([gradient[pl.ds(j, n, stride=stride), :] for j in range(stride)], axis=1)
    )
    tiles = b.shape[0] // n
    for t in range(high.shape[1] // WIDE):
        at = pl.ds(t * WIDE, WIDE)
        p = rows_product(x3, high[:, at], low[:, at])
        for i in range(WIDE // LANES):
            j = t * (WIDE // LANES) + i
            out = a if j < tiles else b
            k = j % tiles
            out[k * n : (k + 1) * n, :] = p[:, i * LANES : (i + 1) * LANES]
    k = tiles * n
    a[k : k + 1, :] = row(jnp.sum(g * g))
    rest = jnp.zeros((TILE - 1, LANES), F32)
    a[k + 1 :, :] = rest if cross is None else rest + cross


def prepare(core, size0, size1, d0, d1, g2, i0, i1, targets, readout, before, gradient, residual, token, sums):
    own = core[0, 0] == 0
    n = targets.shape[0]
    stride = d0.shape[0] // n
    s0, s1 = size0[0:1, :], size1[0:1, :]
    sums[...] = s0 * d0[...] + s1 * d1[...]
    for source, out in ((sums, readout), (d1, before), (g2, gradient)):
        for j in range(stride):
            out[:, pl.ds(j * LANES, LANES)] = own_half_first(
                source[pl.ds(j, n, stride=stride), :], own
            )
    r = targets[...] - s0[:, :1] * i0[...] - s1[:, :1] * i1[...]
    residual[...] = own_half_first(r, own)
    token[...] = jnp.zeros(token.shape, F32)


def finish(core, squares, scal, image, readout_part, before, gradient, residual_part, readout, residual, readout_buf, residual_buf, sems):
    image_sq = jnp.sum(squares[...], axis=0, keepdims=True)
    size = step_size(image_sq, scal)[:, :1]
    beta = scal[1:2, :1]
    parts = sems.shape[0] - 1
    n = readout.shape[0] // parts
    copies = []
    for t in range(parts):
        at = pl.ds(t * n, n)
        readout_buf[at, :] = readout_part[at, :] + size * (gradient[at, :] + beta * before[at, :])
        copies.append(pltpu.make_async_copy(readout_buf.at[at], readout.at[at], sems.at[t]))
        copies[-1].start()
    last = own_half_first(image[...], core[0, 0] == 0)
    residual_buf[...] = residual_part[...] - size * last
    copies.append(pltpu.make_async_copy(residual_buf, residual, sems.at[parts]))
    copies[-1].start()
    for c in copies:
        c.wait()


def shards(states, targets):
    samples, units = states.shape
    outputs = targets.shape[1]
    samp_count = lax.axis_size("samp")
    unit_count = lax.axis_size("unit")
    chips = samp_count // CORES
    half = outputs // CORES
    rows = units // LANES
    vector = shape(TILE, LANES)
    core = jnp.full((1, 1), lax.axis_index("samp") % CORES, jnp.int32)

    swap_cores = [(i, i ^ 1) for i in range(samp_count)]
    blocks = chips // BLOCK
    assert blocks == 4
    groups = [
        [(block * BLOCK + chip) * CORES + c for chip in range(BLOCK)]
        for block in range(blocks)
        for c in range(CORES)
    ]

    def swap(x):
        return lax.ppermute(x, "samp", swap_cores)

    def exchange(x):
        n = x.shape[0]
        x = x.reshape(BLOCK, n // BLOCK, LANES)
        x = lax.all_to_all(x, "samp", 0, 0, axis_index_groups=groups, tiled=True)
        return x.reshape(n, LANES)

    def block_terms(x):
        step = BLOCK * CORES
        return [x] + [
            lax.ppermute(
                x, "samp", [(i, (i + d * step) % samp_count) for i in range(samp_count)]
            )
            for d in range(1, blocks)
        ]

    def sum_samples(pieces, scal):
        n = pieces.shape[0] // BLOCK
        terms = block_terms(call(sum_pieces, shape(n, LANES), exchange(pieces)))
        outs = [shape(half * rows, LANES)] + ([] if scal is None else [vector])
        scals = [] if scal is None else [scal]
        outs = call(sum_blocks, outs, *terms, *scals, rows=rows, copies=BLOCK)
        return outs[0], outs[-1]

    def unit_hop(x, mask):
        return lax.ppermute(x, "unit", [(i, i ^ mask) for i in range(unit_count)])

    def unit_terms(a, b):
        a, b = a + unit_hop(a, 1), b + unit_hop(b, 3)
        return a, unit_hop(a, 3), b, unit_hop(b, 1)

    image_shape = shape(outputs, samples)
    whole = shape(outputs * rows, LANES)
    tiles = outputs * samples // 2 // LANES
    partial = [shape(tiles + TILE, LANES), shape(tiles, LANES)]
    flops = 2 * 4 * samples * units * outputs

    smem = pl.BlockSpec(memory_space=pltpu.SMEM)
    high, low, turned, mine, theirs = call(
        first,
        [shape(samples, units, dtype=BF16)] * 2 + [image_shape] + [shape(half * rows, LANES)] * 2,
        core,
        pltpu.with_memory_space_constraint(states, pltpu.HBM),
        pltpu.with_memory_space_constraint(targets.T, pltpu.HBM),
        specs=[smem, HBM, HBM],
        scratch=[
            pltpu.VMEM((units // FETCH, samples, FETCH), F32),
            pltpu.VMEM((outputs, samples), F32),
            pltpu.SemaphoreType.DMA((units // FETCH + 1,)),
        ],
        limit=32,
        flops=flops,
    )
    high, low = here(high), here(low)
    (high_turned, token), (low_turned, _) = [
        call(turn_states, [shape(units, samples, dtype=BF16), vector], x, flops=flops)
        for x in (high, low)
    ]
    high_turned, low_turned = here(high_turned), here(low_turned)
    pieces = call(add_pieces, shape(half * rows, LANES), mine, swap(theirs), token)
    spread, _ = sum_samples(pieces, None)

    gradients, directions, images, sizes = [], [], [], []
    scal = size = None
    for step in range(ITERS):
        top = exchange(spread)
        bottom = swap(top)
        if step == 0:
            g, *terms = call(
                forward,
                [whole] + partial,
                top,
                bottom,
                high_turned,
                low_turned,
                step=0,
                flops=flops,
            )
        else:
            olds = [gradients[-1]] + ([directions[-1]] if step > 1 else [])
            g, d, *terms = call(
                forward,
                [whole, whole] + partial,
                top,
                bottom,
                size,
                scal,
                *olds,
                high_turned,
                low_turned,
                step=step,
                flops=flops,
            )
            directions.append(d)
        gradients.append(g)
        hops = unit_terms(*terms)
        olds = [images[-1], scal] if step else []
        if step + 1 < ITERS:
            piece = shape(half * (rows + 2), LANES)
            image, scal, mine, theirs = call(
                back,
                [image_shape, vector, piece, piece],
                *hops,
                *olds,
                high,
                low,
                later=step > 0,
                flops=flops,
            )
            images.append(image)
            spread, size = sum_samples(mine + swap(theirs), scal)
            sizes.append(size)
        else:
            *parts, token = call(
                prepare,
                [shape(outputs, units)] * 3 + [image_shape, vector],
                core,
                *sizes,
                *directions,
                gradients[-1],
                *images,
                turned,
                specs=[smem] + [VMEM] * 8,
                scratch=[pltpu.VMEM((outputs * rows, LANES), F32)],
                flops=flops // 4,
            )
            image, scal, squares = call(
                last_image, [image_shape, vector, shape(samp_count, LANES)], *hops, *olds, token
            )
    squares = lax.all_to_all(squares.reshape(samp_count, 1, LANES), "samp", 0, 0, tiled=True)
    squares = squares.reshape(samp_count, LANES)
    readout, residual = call(
        finish,
        [shape(outputs, units), image_shape],
        core,
        squares,
        scal,
        image,
        *parts,
        specs=[smem] + [VMEM] * 7,
        outs=[HBM] * 2,
        scratch=[
            pltpu.VMEM((outputs, units), F32),
            pltpu.VMEM((outputs, samples), F32),
            pltpu.SemaphoreType.DMA((5,)),
        ],
    )
    return readout.T, residual.T


def solution(mesh):
    return jax.shard_map(
        shards,
        mesh=mesh,
        in_specs=(P("samp", "unit"), P("samp", None)),
        out_specs=(P("unit", None), P("samp", None)),
        check_vma=False,
    )
```

```python
import functools

import jax
import jax.numpy as jnp
from jax import lax
from jax.experimental import pallas as pl
from jax.experimental.pallas import tpu as pltpu
from jax.sharding import PartitionSpec as P

ITERS = 3
ridge = 0.5
CORES, BLOCK, LANES, TILE = 2, 8, 128, 8
WIDE, FETCH = 256, 512
MIB = 1 << 20
F32, BF16 = jnp.float32, jnp.bfloat16
VMEM = pl.BlockSpec(memory_space=pltpu.VMEM)
HBM = pl.BlockSpec(memory_space=pl.ANY)


def shape(*dims, dtype=F32):
    return jax.ShapeDtypeStruct(dims, dtype)


def here(x):
    return pltpu.with_memory_space_constraint(x, pltpu.VMEM)


def call(kernel, out_shape, *args, scratch=(), limit=24, specs=None, outs=None, flops=0, **static):
    return pl.pallas_call(
        functools.partial(kernel, **static),
        in_specs=specs or [VMEM] * len(args),
        out_specs=outs or jax.tree.map(lambda _: VMEM, out_shape),
        out_shape=out_shape,
        scratch_shapes=list(scratch),
        compiler_params=pltpu.CompilerParams(vmem_limit_bytes=limit * MIB),
        cost_estimate=pl.CostEstimate(flops=flops, bytes_accessed=MIB, transcendentals=0),
        name=kernel.__name__,
    )(*args)


def split3(x):
    terms = []
    for _ in range(2):
        terms.append(x.astype(BF16))
        x = x - terms[-1].astype(F32)
    return jnp.concatenate(terms + [x.astype(BF16)], axis=0)


def dot(a, b, ca, cb):
    return lax.dot_general(a, b, (((ca,), (cb,)), ((), ())), preferred_element_type=F32)


def rows_product(x3, high, low):
    n = x3.shape[0] // 3
    p = dot(x3[: 2 * n], low, 1, 0)
    q = dot(x3, high, 1, 0)
    return q[:n] + ((p[:n] + q[n : 2 * n]) + (p[n:] + q[2 * n :]))


def row(x):
    return jnp.broadcast_to(x, (1, LANES))


def store_pieces(mine, theirs, value, at, stride):
    half = value.shape[0] // CORES
    for i in range(WIDE // LANES):
        part = value[:, i * LANES : (i + 1) * LANES]
        j = at * (WIDE // LANES) + i
        mine[pl.ds(j, half, stride=stride), :] = part[:half]
        theirs[pl.ds(j, half, stride=stride), :] = part[half:]


def own_half_first(x, own):
    half = x.shape[0] // CORES
    top, bottom = x[:half], x[half:]
    return jnp.concatenate(
        [jnp.where(own, top, bottom), jnp.where(own, bottom, top)], axis=0
    )


def first(core, states, targets, high, low, turned, mine, theirs, buf, target_buf, sems):
    steps = buf.shape[0]
    fetch = pltpu.make_async_copy(targets, target_buf, sems.at[steps])
    fetch.start()
    copies = [
        pltpu.make_async_copy(
            states.at[:, pl.ds(t * FETCH, FETCH)], buf.at[t], sems.at[t]
        )
        for t in range(steps)
    ]
    for c in copies:
        c.start()
    fetch.wait()
    x = own_half_first(target_buf[...], core[0, 0] == 0)
    turned[...] = x
    x3 = split3(x)
    half = x.shape[0] // CORES
    for t in range(steps):
        copies[t].wait()
        s = buf[t]
        h = s.astype(BF16)
        l = (s - h.astype(F32)).astype(BF16)
        high[:, pl.ds(t * FETCH, FETCH)] = h
        low[:, pl.ds(t * FETCH, FETCH)] = l
        p = rows_product(x3, h, l)
        for i in range(FETCH // WIDE):
            part = p[:, i * WIDE : (i + 1) * WIDE]
            store_pieces(mine, theirs, part, t * (FETCH // WIDE) + i, mine.shape[0] // half)


def turn_states(x, turned, token):
    turned[...] = x[...].T
    token[...] = jnp.zeros(token.shape, F32)


def combine(a, ra, b, rb, n):
    tiles = b.shape[0] // n
    parts = []
    for x, rx in ((a, ra), (b, rb)):
        parts += [x[j * n : (j + 1) * n, :] + rx[j * n : (j + 1) * n, :] for j in range(tiles)]
    image = jnp.concatenate(parts, axis=1)
    return image, a[tiles * n :, :] + ra[tiles * n :, :]


def step_image(hops, before, scal, image_out, scal_out):
    image, tail = combine(*hops, image_out.shape[0])
    gamma = tail[0:1]
    if before is None:
        beta = jnp.zeros_like(gamma)
        square = gamma
    else:
        beta = gamma / scal[0:1, :]
        square = gamma + beta * (2.0 * tail[1:2] + beta * scal[2:3, :])
        image = image + beta[:, :1] * before[...]
    image_out[...] = image
    scal_out[0:1, :] = gamma
    scal_out[1:2, :] = beta
    scal_out[2:3, :] = square
    scal_out[3:, :] = jnp.zeros((TILE - 3, LANES), F32)
    return image, row(jnp.sum(image * image))


def back(*refs, later):
    hops = refs[:4]
    before, scal = refs[4:6] if later else (None, None)
    high, low, image_out, scal_out, mine, theirs = refs[-6:]
    image, image_sq = step_image(hops, before, scal, image_out, scal_out)
    half = image.shape[0] // CORES
    stride = mine.shape[0] // half
    x3 = split3(image)
    for t in range(high.shape[1] // WIDE):
        at = pl.ds(t * WIDE, WIDE)
        p = rows_product(x3, high[:, at], low[:, at])
        store_pieces(mine, theirs, p, t, stride)
    extra = jnp.broadcast_to(image_sq, (half, LANES))
    for j in range(high.shape[1] // LANES, stride):
        mine[pl.ds(j, half, stride=stride), :] = extra
        theirs[pl.ds(j, half, stride=stride), :] = extra


def last_image(h0, h1, h2, h3, before, scal, token, image_out, scal_out, squares):
    _, image_sq = step_image((h0, h1, h2, h3), before, scal, image_out, scal_out)
    squares[...] = jnp.broadcast_to(image_sq, squares.shape)


def step_size(image_sq, scal):
    return scal[0:1, :] / (image_sq + ridge * scal[2:3, :])


def add_pieces(a, b, token, out):
    out[...] = a[...] + b[...]


def sum_pieces(got, out):
    n = out.shape[0]
    terms = [got[i * n : (i + 1) * n, :] for i in range(got.shape[0] // n)]
    while len(terms) > 1:
        terms = [terms[i] + terms[i + 1] for i in range(0, len(terms), 2)]
    out[...] = terms[0]


def sum_blocks(*refs, rows, copies):
    t0, t1, t2, t3, *rest = refs
    total = (t0[...] + t2[...]) + (t1[...] + t3[...])
    out = rest[-2] if len(rest) == 3 else rest[-1]
    n = out.shape[0] // copies
    stride = total.shape[0] // (n // rows)
    for i in range(n // rows):
        part = total[i * stride : i * stride + rows]
        for k in range(copies):
            out[k * n + i * rows : k * n + (i + 1) * rows, :] = part
    if len(rest) == 3:
        scal, _, size = rest
        size[...] = jnp.broadcast_to(step_size(total[rows : rows + 1], scal), size.shape)


def forward(*refs, step):
    if step == 0:
        top, bottom, high, low, gradient, a, b = refs
        g = jnp.concatenate([top[...], bottom[...]], axis=0)
        cross = None
    else:
        if step == 1:
            top, bottom, size, scal, g_old, high, low, gradient, direction, a, b = refs
            d = g_old[...]
        else:
            top, bottom, size, scal, g_old, d_old, high, low, gradient, direction, a, b = refs
            d = g_old[...] + scal[1:2, :] * d_old[...]
        q = jnp.concatenate([top[...], bottom[...]], axis=0)
        direction[...] = d
        g = g_old[...] - size[0:1, :] * (q + ridge * d)
        cross = jnp.sum(g * d)
    gradient[...] = g
    stride = high.shape[0] // LANES
    n = g.shape[0] // stride
    x3 = split3(
        jnp.concatenate([gradient[pl.ds(j, n, stride=stride), :] for j in range(stride)], axis=1)
    )
    tiles = b.shape[0] // n
    for t in range(high.shape[1] // WIDE):
        at = pl.ds(t * WIDE, WIDE)
        p = rows_product(x3, high[:, at], low[:, at])
        for i in range(WIDE // LANES):
            j = t * (WIDE // LANES) + i
            out = a if j < tiles else b
            k = j % tiles
            out[k * n : (k + 1) * n, :] = p[:, i * LANES : (i + 1) * LANES]
    k = tiles * n
    a[k : k + 1, :] = row(jnp.sum(g * g))
    rest = jnp.zeros((TILE - 1, LANES), F32)
    a[k + 1 :, :] = rest if cross is None else rest + cross


def prepare(core, size0, size1, d0, d1, g2, i0, i1, targets, readout, before, gradient, residual, token, sums):
    own = core[0, 0] == 0
    n = targets.shape[0]
    stride = d0.shape[0] // n
    s0, s1 = size0[0:1, :], size1[0:1, :]
    sums[...] = s0 * d0[...] + s1 * d1[...]
    for source, out in ((sums, readout), (d1, before), (g2, gradient)):
        for j in range(stride):
            out[:, pl.ds(j * LANES, LANES)] = own_half_first(
                source[pl.ds(j, n, stride=stride), :], own
            )
    r = targets[...] - s0[:, :1] * i0[...] - s1[:, :1] * i1[...]
    residual[...] = own_half_first(r, own)
    token[...] = jnp.zeros(token.shape, F32)


def finish(core, squares, scal, image, readout_part, before, gradient, residual_part, readout, residual, readout_buf, residual_buf, sems):
    image_sq = jnp.sum(squares[...], axis=0, keepdims=True)
    size = step_size(image_sq, scal)[:, :1]
    beta = scal[1:2, :1]
    parts = sems.shape[0] - 1
    n = readout.shape[0] // parts
    copies = []
    for t in range(parts):
        at = pl.ds(t * n, n)
        readout_buf[at, :] = readout_part[at, :] + size * (gradient[at, :] + beta * before[at, :])
        copies.append(pltpu.make_async_copy(readout_buf.at[at], readout.at[at], sems.at[t]))
        copies[-1].start()
    last = own_half_first(image[...], core[0, 0] == 0)
    residual_buf[...] = residual_part[...] - size * last
    copies.append(pltpu.make_async_copy(residual_buf, residual, sems.at[parts]))
    copies[-1].start()
    for c in copies:
        c.wait()


def shards(states, targets):
    samples, units = states.shape
    outputs = targets.shape[1]
    samp_count = lax.axis_size("samp")
    unit_count = lax.axis_size("unit")
    chips = samp_count // CORES
    half = outputs // CORES
    rows = units // LANES
    vector = shape(TILE, LANES)
    core = jnp.full((1, 1), lax.axis_index("samp") % CORES, jnp.int32)

    swap_cores = [(i, i ^ 1) for i in range(samp_count)]
    blocks = chips // BLOCK
    assert blocks == 4
    groups = [
        [(block * BLOCK + chip) * CORES + c for chip in range(BLOCK)]
        for block in range(blocks)
        for c in range(CORES)
    ]

    def swap(x):
        return lax.ppermute(x, "samp", swap_cores)

    def exchange(x):
        n = x.shape[0]
        x = x.reshape(BLOCK, n // BLOCK, LANES)
        x = lax.all_to_all(x, "samp", 0, 0, axis_index_groups=groups, tiled=True)
        return x.reshape(n, LANES)

    def block_terms(x):
        step = BLOCK * CORES
        return [x] + [
            lax.ppermute(
                x, "samp", [(i, (i + d * step) % samp_count) for i in range(samp_count)]
            )
            for d in range(1, blocks)
        ]

    def sum_samples(pieces, scal, tokens=()):
        n = pieces.shape[0] // BLOCK
        terms = block_terms(call(sum_pieces, shape(n, LANES), exchange(pieces)))
        outs = [shape(half * rows, LANES)] + ([] if scal is None else [vector])
        scals = list(tokens) if scal is None else [scal]
        outs = call(sum_blocks, outs, *terms, *scals, rows=rows, copies=BLOCK)
        return outs[0], outs[-1]

    def unit_hop(x, mask):
        return lax.ppermute(x, "unit", [(i, i ^ mask) for i in range(unit_count)])

    def unit_terms(a, b):
        a, b = a + unit_hop(a, 1), b + unit_hop(b, 3)
        return a, unit_hop(a, 3), b, unit_hop(b, 1)

    image_shape = shape(outputs, samples)
    whole = shape(outputs * rows, LANES)
    tiles = outputs * samples // 2 // LANES
    partial = [shape(tiles + TILE, LANES), shape(tiles, LANES)]
    flops = 2 * 4 * samples * units * outputs

    smem = pl.BlockSpec(memory_space=pltpu.SMEM)
    high, low, turned, mine, theirs = call(
        first,
        [shape(samples, units, dtype=BF16)] * 2 + [image_shape] + [shape(half * rows, LANES)] * 2,
        core,
        pltpu.with_memory_space_constraint(states, pltpu.HBM),
        pltpu.with_memory_space_constraint(targets.T, pltpu.HBM),
        specs=[smem, HBM, HBM],
        scratch=[
            pltpu.VMEM((units // FETCH, samples, FETCH), F32),
            pltpu.VMEM((outputs, samples), F32),
            pltpu.SemaphoreType.DMA((units // FETCH + 1,)),
        ],
        limit=32,
        flops=flops,
    )
    high, low = here(high), here(low)
    (high_turned, token), (low_turned, token_low) = [
        call(turn_states, [shape(units, samples, dtype=BF16), vector], x, flops=flops)
        for x in (high, low)
    ]
    high_turned, low_turned = here(high_turned), here(low_turned)
    pieces = call(add_pieces, shape(half * rows, LANES), mine, swap(theirs), token)
    spread, _ = sum_samples(pieces, None, [token_low])

    gradients, directions, images, sizes = [], [], [], []
    scal = size = None
    for step in range(ITERS):
        top = exchange(spread)
        bottom = swap(top)
        if step == 0:
            g, *terms = call(
                forward,
                [whole] + partial,
                top,
                bottom,
                high_turned,
                low_turned,
                step=0,
                flops=flops,
            )
        else:
            olds = [gradients[-1]] + ([directions[-1]] if step > 1 else [])
            g, d, *terms = call(
                forward,
                [whole, whole] + partial,
                top,
                bottom,
                size,
                scal,
                *olds,
                high_turned,
                low_turned,
                step=step,
                flops=flops,
            )
            directions.append(d)
        gradients.append(g)
        hops = unit_terms(*terms)
        olds = [images[-1], scal] if step else []
        if step + 1 < ITERS:
            piece = shape(half * (rows + 2), LANES)
            image, scal, mine, theirs = call(
                back,
                [image_shape, vector, piece, piece],
                *hops,
                *olds,
                high,
                low,
                later=step > 0,
                flops=flops,
            )
            images.append(image)
            spread, size = sum_samples(mine + swap(theirs), scal)
            sizes.append(size)
        else:
            *parts, token = call(
                prepare,
                [shape(outputs, units)] * 3 + [image_shape, vector],
                core,
                *sizes,
                *directions,
                gradients[-1],
                *images,
                turned,
                specs=[smem] + [VMEM] * 8,
                scratch=[pltpu.VMEM((outputs * rows, LANES), F32)],
                flops=flops // 4,
            )
            image, scal, squares = call(
                last_image, [image_shape, vector, shape(samp_count, LANES)], *hops, *olds, token
            )
    squares = lax.all_to_all(squares.reshape(samp_count, 1, LANES), "samp", 0, 0, tiled=True)
    squares = squares.reshape(samp_count, LANES)
    readout, residual = call(
        finish,
        [shape(outputs, units), image_shape],
        core,
        squares,
        scal,
        image,
        *parts,
        specs=[smem] + [VMEM] * 7,
        outs=[HBM] * 2,
        scratch=[
            pltpu.VMEM((outputs, units), F32),
            pltpu.VMEM((outputs, samples), F32),
            pltpu.SemaphoreType.DMA((5,)),
        ],
    )
    return readout.T, residual.T


def solution(mesh):
    return jax.shard_map(
        shards,
        mesh=mesh,
        in_specs=(P("samp", "unit"), P("samp", None)),
        out_specs=(P("unit", None), P("samp", None)),
        check_vma=False,
    )
```
